256 devices in a mesh: shot: 8 (over y, x_hi), gx: 4 (over x_lo, core), gy: 8 (over z).
Axes of the slice: x: 4 (x_hi: 2, x_lo: 2; x = x_hi * 2 + x_lo), y: 4, z: 8, core: 2. Of those that a mesh axis runs over, the one named last changes fastest.
Arguments:
- speed_squared: float32 [192, 64, 256], P('gx', 'gy'), may hold values from 0.04 to 0.12
- epsilon_term: float32 [192, 64, 256], P('gx', 'gy'), may hold values from 1 to 1.5
- delta_term: float32 [192, 64, 256], P('gx', 'gy'), may hold values from 0.9 to 1.2
- tilt_term: float32 [192, 64, 256], P('gx', 'gy'), may hold values from -0.1 to 0.1
- perturbation: float32 [3, 192, 64, 256], P(None, 'gx', 'gy', 'shot'), may hold values from -6 to 6
- forward_prev: float32 [8, 192, 64, 256], P('shot', 'gx', 'gy'), may hold values from -1.8 to 1.8
- forward_now: float32 [8, 192, 64, 256], P('shot', 'gx', 'gy'), may hold values from -1.8 to 1.8
- adjoint_prev: float32 [8, 192, 64, 256], P('shot', 'gx', 'gy'), may hold values from -1.8 to 1.8
- adjoint_now: float32 [8, 192, 64, 256], P('shot', 'gx', 'gy'), may hold values from -1.8 to 1.8
- wavelet: float32 [8, 2], P('shot'), may hold values from 0.5 to 2
- source_cell: int32 [8], P('shot'), may hold values from 0 to 255
- receiver_cells: int32 [8, 1536], P('shot'), may hold values from 0 to 3145727
Outputs:
- hessian_product: float32 [3, 192, 64, 256], P(None, 'gx', 'gy', 'shot')
The draws below stay inside these ranges and needn't reach their ends.
Inputs may be any that keep to these rules, and one draw needn't show every extreme that they name: `source_cell`: the depth index z of the group's horizontal plane source. `receiver_cells`: flattened cell indices x * 64 * 256 + y * 256 + z; several receivers may share a cell.
All inputs are finite; a program needn't handle non-finite values.
Results may differ from the reference program's by a relative error of at most 0.00002.
Values sent between devices are 32-bit elements; how exact they have to be, the bound alone decides.
No kernel may reach another device: no remote copies, remote signals or barrier semaphores. Data moves between devices by JAX's collectives and lax.ppermute only.
A program may use at most 192 MiB of HBM per device.

```python
import math
import jax
import jax.numpy as jnp

NZ = 256
NT = 2
NSHOT = 8
AX = 192
AY = 64
NREC = 1536


def plant(values, own_key, low, largest):
    dims = values.shape
    index_at = [jax.random.randint(jax.random.fold_in(own_key, axis), (), 0, dims[axis]) for axis in range(len(dims))]
    values = values.at[tuple(index_at)].set(low)
    longest = dims.index(max(dims))
    index_at[longest] = (index_at[longest] + 1) % dims[longest]
    return values.at[tuple(index_at)].set(largest)


def with_spikes(result, own_key, source, target, blocks, factor):
    def block_of(dim):
        return (jnp.arange(result.shape[dim]) // (result.shape[dim] // blocks)).reshape((-1,) + (1,) * (result.ndim - 1 - dim))

    first = jax.random.permutation(own_key, blocks)[block_of(target)]
    other_side = (block_of(target) + blocks // 2) % blocks
    return jnp.where((block_of(source) == first) | (block_of(source) == other_side), factor * result, result)


def steps_of(own_key, shape, shards, low, high):
    def one(dim, shards_of):
        steps = jax.random.uniform(jax.random.fold_in(jax.random.fold_in(own_key, 6), dim), (shards_of,), jnp.float32, low / len(shards), high / len(shards))
        return jnp.repeat(jnp.exp(steps), shape[dim] // shards_of).reshape((-1,) + (1,) * (len(shape) - dim - 1))

    factor_of = one(*shards[0])
    for cut in shards[1:]:
        factor_of = factor_of * one(*cut)
    return factor_of


def bell_draw(rng, dims, deviation, bound, split=(), kind=jnp.bfloat16):
    values = deviation * jax.random.normal(rng, dims, jnp.float32)
    if split:
        values = values * steps_of(rng, dims, split, -0.22, 0.18)
    return jnp.clip(values, -bound, bound).astype(kind)


def bell_draw_with(key, shape, deviation, reach, pieces, heavy, held_as=jnp.bfloat16):
    entries = deviation * jax.random.normal(key, shape, jnp.float32)
    if pieces:
        entries = entries * steps_of(key, shape, pieces, -0.22, 0.18)
    return jnp.clip(with_spikes(entries, jax.random.fold_in(key, 3), *heavy), -reach, reach).astype(held_as)


def setup_inputs(seed: int = 0) -> dict:
    keys = jax.random.split(jax.random.key(seed), 13)
    return {
        "speed_squared": jnp.clip(jnp.exp(math.log(0.12) - 1.0986123 * jax.random.uniform(keys[0], (AX, AY, NZ), jnp.float32) ** steps_of(keys[0], (AX, AY, NZ), ((0, 4), (1, 8)), -0.2, 0.2)), 0.04, 0.12),
        "epsilon_term": jnp.clip(1.0 + 0.5 * jax.random.uniform(keys[1], (AX, AY, NZ), jnp.float32) ** steps_of(keys[1], (AX, AY, NZ), ((0, 4), (1, 8)), -0.2, 0.2), 1.0, 1.5),
        "delta_term": jnp.clip(0.9 + 0.30000007 * jax.random.uniform(keys[2], (AX, AY, NZ), jnp.float32) ** steps_of(keys[2], (AX, AY, NZ), ((0, 4), (1, 8)), -0.2, 0.2), 0.9, 1.2),
        "tilt_term": jnp.clip(jax.random.uniform(keys[3], (AX, AY, NZ), jnp.float32, -0.1, 0.1) * steps_of(keys[3], (AX, AY, NZ), ((0, 4), (1, 8)), -0.4, 0.0), -0.1, 0.1),
        "perturbation": bell_draw(keys[4], (3, AX, AY, NZ), 1.0, 6.0, ((1, 4), (2, 8), (3, 8)), jnp.float32),
        "forward_prev": bell_draw(keys[5], (NSHOT, AX, AY, NZ), 0.3, 1.8, ((0, 8), (1, 4), (2, 8)), jnp.float32),
        "forward_now": bell_draw(keys[6], (NSHOT, AX, AY, NZ), 0.3, 1.8, ((0, 8), (1, 4), (2, 8)), jnp.float32),
        "adjoint_prev": bell_draw(keys[7], (NSHOT, AX, AY, NZ), 0.3, 1.8, ((0, 8), (1, 4), (2, 8)), jnp.float32),
        "adjoint_now": bell_draw_with(keys[8], (NSHOT, AX, AY, NZ), 0.3, 1.8, ((0, 8), (1, 4), (2, 8)), (0, 3, 8, 2.0), jnp.float32),
        "wavelet": jnp.clip(jnp.exp(math.log(2.0) - 1.3862944 * jax.random.uniform(keys[9], (NSHOT, NT), jnp.float32) ** steps_of(keys[9], (NSHOT, NT), ((0, 8),), -0.2, 0.2)), 0.5, 2.0),
        "source_cell": plant(jax.random.randint(keys[10], (NSHOT,), 0, NZ), jax.random.fold_in(keys[10], 1), 0, NZ - 1).astype(jnp.int32),
        "receiver_cells": plant(jax.random.randint(keys[11], (NSHOT, NREC), 0, AX * AY * NZ), jax.random.fold_in(keys[11], 1), 0, (AX * AY * NZ) - 1).astype(jnp.int32),
    }


second_weights = (-1.0 / 12.0, 4.0 / 3.0, -2.5, 4.0 / 3.0, -1.0 / 12.0)
first_weights = (1.0 / 12.0, -2.0 / 3.0, 0.0, 2.0 / 3.0, -1.0 / 12.0)


def widen(field):
    return jnp.pad(field, ((2, 2), (2, 2), (0, 0)))


def derivs(padded):
    size_x = padded.shape[0] - 4
    size_y = padded.shape[1] - 4
    size_z = padded.shape[2]
    padded_z = jnp.pad(padded, ((0, 0), (0, 0), (2, 2)))
    horizontal = 0.0
    vertical = 0.0
    vertical_slope = 0.0
    for offset in range(5):
        horizontal = horizontal + second_weights[offset] * (padded_z[offset:offset + size_x, 2:2 + size_y, 2:2 + size_z] + padded_z[2:2 + size_x, offset:offset + size_y, 2:2 + size_z])
        vertical = vertical + second_weights[offset] * padded_z[2:2 + size_x, 2:2 + size_y, offset:offset + size_z]
        vertical_slope = vertical_slope + first_weights[offset] * padded_z[:, :, offset:offset + size_z]
    mixed_term = 0.0
    for offset in range(5):
        mixed_term = mixed_term + first_weights[offset] * (vertical_slope[offset:offset + size_x, 2:2 + size_y] + vertical_slope[2:2 + size_x, offset:offset + size_y])
    return horizontal, vertical, mixed_term


def operate(parts, speed, epsilon, delta, tilt):
    return speed * (epsilon * parts[0] + delta * parts[1]) + tilt * parts[2]


def born_source(parts, speed, epsilon, delta, change):
    return change[0] * (epsilon * parts[0] + delta * parts[1]) + speed * (change[1] * parts[0] + change[2] * parts[1])


def imaging(parts, speed, epsilon, delta):
    return jnp.stack([epsilon * parts[0] + delta * parts[1], speed * parts[0], speed * parts[1]])


def reference(speed_squared, epsilon_term, delta_term, tilt_term, perturbation, forward_prev, forward_now, adjoint_prev, adjoint_now, wavelet, source_cell, receiver_cells):
    speed, epsilon, delta, tilt = speed_squared, epsilon_term, delta_term, tilt_term
    total = jnp.zeros((3, AX, AY, NZ), jnp.float32)
    depth_index = jnp.arange(NZ, dtype=jnp.int32)
    for group in range(NSHOT):
        counts = jnp.zeros((AX * AY * NZ,), jnp.float32).at[receiver_cells[group]].add(1.0).reshape(AX, AY, NZ)
        plane = jnp.where(depth_index == source_cell[group], 1.0, 0.0).astype(jnp.float32)
        u_prev, u_curr = forward_prev[group], forward_now[group]
        l_prev, l_curr = adjoint_prev[group], adjoint_now[group]
        b_prev = jnp.zeros((AX, AY, NZ), jnp.float32)
        b_curr = b_prev
        d_prev = b_prev
        d_curr = b_prev
        parts_u = derivs(widen(u_curr))
        parts_b = derivs(widen(b_curr))
        for level in range(NT):
            parts_l = derivs(widen(l_curr))
            parts_d = derivs(widen(d_curr))
            u_next = 2.0 * u_curr - u_prev + operate(parts_u, speed, epsilon, delta, tilt)
            u_next = u_next + wavelet[group, level] * plane
            b_next = 2.0 * b_curr - b_prev + operate(parts_b, speed, epsilon, delta, tilt) + born_source(parts_u, speed, epsilon, delta, perturbation)
            l_next = 2.0 * l_curr - l_prev + operate(parts_l, speed, epsilon, delta, tilt)
            d_next = 2.0 * d_curr - d_prev + operate(parts_d, speed, epsilon, delta, tilt) + born_source(parts_l, speed, epsilon, delta, perturbation) + counts * b_curr
            parts_u = derivs(widen(u_next))
            parts_b = derivs(widen(b_next))
            total = total + imaging(parts_u, speed, epsilon, delta) * d_next + imaging(parts_b, speed, epsilon, delta) * l_next
            u_prev, u_curr = u_curr, u_next
            b_prev, b_curr = b_curr, b_next
            l_prev, l_curr = l_curr, l_next
            d_prev, d_curr = d_curr, d_next
    return total
```

```python
import functools

import jax
import jax.numpy as jnp
from jax import lax
from jax.experimental import pallas as pl
from jax.experimental.pallas import tpu as pltpu
from jax.sharding import PartitionSpec as P

F32 = jnp.float32
VM = pl.BlockSpec(memory_space=pltpu.VMEM)
SM = pl.BlockSpec(memory_space=pltpu.SMEM)
LIMIT = 24 * 1024 * 1024

S0, S1, S2 = -2.5, 4.0 / 3.0, -1.0 / 12.0
D1, D2 = 2.0 / 3.0, -1.0 / 12.0


def call(kernel, outs, ins, scratch=(), smem=(), cost=None, name=None):
    return pl.pallas_call(
        kernel,
        out_shape=[jax.ShapeDtypeStruct(shape, F32) for shape in outs],
        in_specs=[SM if i in smem else VM for i in range(len(ins))],
        out_specs=[VM] * len(outs),
        scratch_shapes=list(scratch),
        compiler_params=pltpu.CompilerParams(vmem_limit_bytes=LIMIT),
        cost_estimate=cost,
        name=name,
    )(*ins)


def cycle(value, axis, step):
    size = lax.axis_size(axis)
    return lax.ppermute(value, axis, [(i, (i + step) % size) for i in range(size)])


def rows():
    return lax.broadcasted_iota(jnp.int32, (8, 128), 0)


def lanes():
    return lax.broadcasted_iota(jnp.int32, (8, 128), 1)


def pack_y(fields, up, down):
    row = rows()
    nx = fields[0].shape[0]
    pieces = 4 // len(fields)
    step = nx // pieces

    def body(i, _):
        for h in (0, 128):
            tile = pl.ds(h, 128)
            for out, base in ((up, 6), (down, 0)):
                acc = None
                for piece in range(pieces):
                    for f, field in enumerate(fields):
                        at = 2 * (piece * len(fields) + f)
                        value = field[i + piece * step, :, tile]
                        value = pltpu.roll(value, (at - base) % 8, 0) if at != base else value
                        acc = value if acc is None else jnp.where(row >= at, value, acc)
                out[i, :, tile] = acc
        return 0

    lax.fori_loop(0, step, body, 0, unroll=2)


def pack_x(fields, up, down):
    for f, field in enumerate(fields):
        n = field.shape[0]
        up[2 * f : 2 * f + 2] = field[n - 2 : n]
        down[2 * f : 2 * f + 2] = field[0:2]


def fill(pad, field, before, after, f, gx, last_x):
    n = field.shape[0]
    pad[2 : n + 2] = field[...]
    pad[0:2] = jnp.where(gx > 0, before[2 * f : 2 * f + 2], 0.0)
    pad[n + 2 : n + 4] = jnp.where(gx < last_x, after[2 * f : 2 * f + 2], 0.0)


def edge_rows(before, after, i, at, tile, first, last):
    row = rows()
    lower = before[i, :, tile]
    upper = after[i, :, tile]
    if at != 6:
        lower = pltpu.roll(lower, (6 - at) % 8, 0)
    if at != 0:
        upper = pltpu.roll(upper, (-at) % 8, 0)
    return jnp.where((row >= 6) & first, lower, jnp.where((row <= 1) & last, upper, 0.0))


def z_shifts(a, b):
    lane = lanes()
    out = []
    for k in (1, 2):
        ra, rb = pltpu.roll(a, k, 1), pltpu.roll(b, k, 1)
        low = (jnp.where(lane < k, 0.0, ra), jnp.where(lane < k, ra, rb))
        ra, rb = pltpu.roll(a, 128 - k, 1), pltpu.roll(b, 128 - k, 1)
        high = (jnp.where(lane >= 128 - k, rb, ra), jnp.where(lane >= 128 - k, 0.0, rb))
        out.append((low, high))
    return out


def second_z(pair):
    (l1, h1), (l2, h2) = z_shifts(*pair)
    return [S0 * pair[t] + S1 * (l1[t] + h1[t]) + S2 * (l2[t] + h2[t]) for t in (0, 1)]


def first_z(pair):
    (l1, h1), (l2, h2) = z_shifts(*pair)
    return [D1 * (h1[t] - l1[t]) + D2 * (h2[t] - l2[t]) for t in (0, 1)]


def lateral(pad, x, edge, slope=True):
    row = rows()
    horizontal, slopes, centre = [], [], []
    for t in (0, 1):
        tile = pl.ds(128 * t, 128)
        c = pad[x + 2, :, tile]
        xl, xh, xl2, xh2 = (pad[x + k, :, tile] for k in (1, 3, 0, 4))
        e = edge[t]
        yl = pltpu.roll(jnp.where(row == 7, e, c), 1, 0)
        yl2 = pltpu.roll(jnp.where(row >= 6, e, c), 2, 0)
        yh = pltpu.roll(jnp.where(row == 0, e, c), 7, 0)
        yh2 = pltpu.roll(jnp.where(row <= 1, e, c), 6, 0)
        horizontal.append(2.0 * S0 * c + S1 * ((xl + xh) + (yl + yh)) + S2 * ((xl2 + xh2) + (yl2 + yh2)))
        if slope:
            slopes.append(D1 * ((xh - xl) + (yh - yl)) + D2 * ((xh2 - xl2) + (yh2 - yl2)))
        centre.append(c)
    return horizontal, slopes, centre


def derivs(pad, x, edge):
    horizontal, slopes, centre = lateral(pad, x, edge)
    return horizontal, second_z(centre), first_z(slopes), centre


def places():
    return lax.axis_index("gx"), lax.axis_index("gy")


def chunk_of(array, shot, lane_shift):
    half = array[:, :, pl.ds(pl.multiple_of((shot // 4) * 128, 128), 128)]
    return pltpu.roll(half, lane_shift, 2)


def prepare_kernel(u, l, p, speed, epsilon, delta, yup, ydn, xup, xdn, chunk, model, pbuf):
    fields = [u.at[0], l.at[0]]
    pack_y(fields, yup, ydn)
    pack_x(fields, xup, xdn)
    shot = lax.axis_index("shot")
    shift = lax.rem(128 - 32 * lax.rem(shot, 4), 128)
    for k, array in enumerate((speed, epsilon, delta)):
        model[k] = chunk_of(array, shot, shift)
    pbuf[:, :, :, 0:32] = p[...]
    lane = lanes()
    group = p.shape[1] // 4
    for i in range(group):
        parts = [[], []]
        for g in range(4):
            x = g * group + i
            p0, p1, p2 = (pbuf[k, x] for k in range(3))
            s, e, d = (model[k, x] for k in range(3))
            for f, q in enumerate((p0 * e + s * p1, p0 * d + s * p2)):
                parts[f].append(pltpu.roll(q, 32 * g, 1) if g else q)
        for f in (0, 1):
            a, b, c, d = parts[f]
            chunk[f * group + i] = jnp.where(
                lane < 32, a, jnp.where(lane < 64, b, jnp.where(lane < 96, c, d))
            )


def first_kernel(
    wavelet, source, u, um, l, lm, ylo, yhi, xlo, xhi, speed, epsilon, delta, tilt,
    u1, l1, hu, vu, hl, vl, padu, padl,
):
    gx, gy = places()
    first, last = gy > 0, gy < lax.axis_size("gy") - 1
    for f, (pad, w) in enumerate(((padu, u), (padl, l))):
        fill(pad, w.at[0], xlo, xhi, f, gx, lax.axis_size("gx") - 1)
    nx = u.shape[1]
    half = nx // 2
    lane = lanes()
    amount, depth = wavelet[0, 0], source[0]
    for piece in (0, 1):

        def body(i, _):
            x = i + piece * half
            for f, (pad, prev, nxt, h_out, v_out) in enumerate(
                ((padu, um, u1, hu, vu), (padl, lm, l1, hl, vl))
            ):
                edge = [
                    edge_rows(ylo, yhi, i, 4 * piece + 2 * f, pl.ds(128 * t, 128), first, last)
                    for t in (0, 1)
                ]
                hh, vv, mm, cc = derivs(pad, x, edge)
                for t in (0, 1):
                    tile = pl.ds(128 * t, 128)
                    h_out[x, :, tile] = hh[t]
                    v_out[x, :, tile] = vv[t]
                    new = 2.0 * cc[t] - prev[0, x, :, tile] + (
                        speed[x, :, tile] * (epsilon[x, :, tile] * hh[t] + delta[x, :, tile] * vv[t])
                        + tilt[x, :, tile] * mm[t]
                    )
                    if f == 0:
                        new = new + jnp.where(lane + 128 * t == depth, amount, 0.0)
                    nxt[x, :, tile] = new
            return 0

        lax.fori_loop(0, half, body, 0, unroll=2)


def born_kernel(
    mine, from1, from2, from3, u1, l1, hu, vu, hl, vl,
    q1, q2, b1, d1, yup, ydn, xup, xdn, chunks,
):
    shot = lax.axis_index("shot")
    y, xh = shot // 2, lax.rem(shot, 2)
    group = u1.shape[0] // 4
    for k, pair in enumerate((mine, from1, from2, from3)):
        there = lax.rem(y + 4 - k, 4) * 2
        chunks[there + xh] = pair[0 : 2 * group]
        chunks[there + 1 - xh] = pair[2 * group : 4 * group]
    lane = lanes()
    for g in range(4):

        def body(i, _):
            x = g * group + i
            for t in (0, 1):
                tile = pl.ds(128 * t, 128)
                both = []
                for f in (0, 1):
                    parts = []
                    for k in range(4):
                        part = chunks[4 * t + k, f * group + i]
                        parts.append(pltpu.roll(part, (32 * (k - g)) % 128, 1) if k != g else part)
                    a, b, c, d = parts
                    both.append(jnp.where(lane < 32, a, jnp.where(lane < 64, b, jnp.where(lane < 96, c, d))))
                q1[x, :, tile], q2[x, :, tile] = both
                b1[x, :, tile] = both[0] * hu[x, :, tile] + both[1] * vu[x, :, tile]
                d1[x, :, tile] = both[0] * hl[x, :, tile] + both[1] * vl[x, :, tile]
            return 0

        lax.fori_loop(0, group, body, 0, unroll=2)
    fields = [u1, b1, l1, d1]
    pack_y(fields, yup, ydn)
    pack_x(fields, xup, xdn)


def second_kernel(
    wavelet, source, u, u1, b1, q1, q2, ylo, yhi, xlo, xhi, speed, epsilon, delta, tilt,
    u2, b2, hu, vu, hb, vb, yup, ydn, xup, xdn, padu, padb,
):
    gx, gy = places()
    first, last = gy > 0, gy < lax.axis_size("gy") - 1
    for f, (pad, w) in enumerate(((padu, u1), (padb, b1))):
        fill(pad, w, xlo, xhi, f, gx, lax.axis_size("gx") - 1)
    lane = lanes()
    amount, depth = wavelet[0, 1], source[0]

    def body(x, _):
        edges = [
            [edge_rows(ylo, yhi, x, 2 * f, pl.ds(128 * t, 128), first, last) for t in (0, 1)] for f in (0, 1)
        ]
        h0, v0, m0, c0 = derivs(padu, x, edges[0])
        h1, v1, m1, c1 = derivs(padb, x, edges[1])
        for t in (0, 1):
            tile = pl.ds(128 * t, 128)
            s, e, d, k = (w[x, :, tile] for w in (speed, epsilon, delta, tilt))
            u2[x, :, tile] = (
                2.0 * c0[t] - u[0, x, :, tile] + (s * (e * h0[t] + d * v0[t]) + k * m0[t])
                + jnp.where(lane + 128 * t == depth, amount, 0.0)
            )
            b2[x, :, tile] = (
                2.0 * c1[t] + (s * (e * h1[t] + d * v1[t]) + k * m1[t])
                + (q1[x, :, tile] * h0[t] + q2[x, :, tile] * v0[t])
            )
            hu[x, :, tile], vu[x, :, tile] = h0[t], v0[t]
            hb[x, :, tile], vb[x, :, tile] = h1[t], v1[t]
        return 0

    lax.fori_loop(0, u1.shape[0], body, 0, unroll=2)
    fields = [u2, b2]
    pack_y(fields, yup, ydn)
    pack_x(fields, xup, xdn)


def counts_kernel(cells, out, *, size_y, depth):
    nx, ny = out.shape[0], out.shape[1]
    gx, gy = places()
    index = cells[...]
    cx = lax.div(index, size_y * depth) - gx * nx
    cy = lax.rem(lax.div(index, depth), size_y) - gy * ny
    cz = lax.rem(index, depth)
    inside = (cx >= 0) & (cx < nx) & (cy >= 0) & (cy < ny)
    place = jnp.where(inside, cx * ny + cy, -1)
    n = index.shape[1]
    left = jnp.where(lax.broadcasted_iota(jnp.int32, (nx * ny, n), 0) == place, 1.0, 0.0).astype(jnp.bfloat16)
    right = jnp.where(lax.broadcasted_iota(jnp.int32, (depth, n), 0) == cz, 1.0, 0.0).astype(jnp.bfloat16)
    total = lax.dot_general(left, right, (((1,), (1,)), ((), ())), preferred_element_type=F32)
    out[...] = total.reshape(nx, ny, depth)


def adjoint_kernel(
    l, l1, d1, b1, q1, q2, counts, hu, vu, hb, vb, u2, b2, ylo, yhi, xlo, xhi, speed, epsilon, delta, tilt,
    l2, d2, a1, c1, padl, padd,
):
    gx, gy = places()
    first, last = gy > 0, gy < lax.axis_size("gy") - 1
    for f, (pad, w) in enumerate(((padl, l1), (padd, d1))):
        fill(pad, w, xlo, xhi, f + 2, gx, lax.axis_size("gx") - 1)

    def body(x, _):
        edges = [
            [edge_rows(ylo, yhi, x, 4 + 2 * f, pl.ds(128 * t, 128), first, last) for t in (0, 1)]
            for f in (0, 1)
        ]
        hl, vl, ml, cl = derivs(padl, x, edges[0])
        hd, vd, md, cd = derivs(padd, x, edges[1])
        vu2 = second_z([u2[x, :, pl.ds(128 * t, 128)] for t in (0, 1)])
        vb2 = second_z([b2[x, :, pl.ds(128 * t, 128)] for t in (0, 1)])
        for t in (0, 1):
            tile = pl.ds(128 * t, 128)
            s, e, d, k = (w[x, :, tile] for w in (speed, epsilon, delta, tilt))
            new_l = 2.0 * cl[t] - l[0, x, :, tile] + (s * (e * hl[t] + d * vl[t]) + k * ml[t])
            new_d = (
                2.0 * cd[t] + (s * (e * hd[t] + d * vd[t]) + k * md[t])
                + (q1[x, :, tile] * hl[t] + q2[x, :, tile] * vl[t]) + counts[x, :, tile] * b1[x, :, tile]
            )
            l2[x, :, tile] = new_l
            d2[x, :, tile] = new_d
            a1[x, :, tile] = hu[x, :, tile] * cd[t] + hb[x, :, tile] * cl[t]
            c1[x, :, tile] = (
                vu[x, :, tile] * cd[t] + vb[x, :, tile] * cl[t] + vu2[t] * new_d + vb2[t] * new_l
            )
        return 0

    lax.fori_loop(0, l1.shape[0], body, 0, unroll=2)


def image_kernel(u2, b2, ylo, yhi, xlo, xhi, l2, d2, a1, c1, *rest):
    outs, (padu, padb, total, chunks) = rest[:8], rest[8:]
    gx, gy = places()
    first, last = gy > 0, gy < lax.axis_size("gy") - 1
    for f, (pad, w) in enumerate(((padu, u2), (padb, b2))):
        fill(pad, w, xlo, xhi, f, gx, lax.axis_size("gx") - 1)
    nx = u2.shape[0]
    half = nx // 2
    for piece in (0, 1):

        def body(i, _):
            x = i + piece * half
            edges = [
                [
                    edge_rows(ylo, yhi, i, 4 * piece + 2 * f, pl.ds(128 * t, 128), first, last)
                    for t in (0, 1)
                ]
                for f in (0, 1)
            ]
            hu = lateral(padu, x, edges[0], False)[0]
            hb = lateral(padb, x, edges[1], False)[0]
            for t in (0, 1):
                tile = pl.ds(128 * t, 128)
                total[x, :, tile] = a1[x, :, tile] + hu[t] * d2[x, :, tile] + hb[t] * l2[x, :, tile]
            return 0

        lax.fori_loop(0, half, body, 0, unroll=2)
    lane = lanes()
    group = nx // 4

    def pack(i, _):
        for f, array in enumerate((total, c1)):
            for t in (0, 1):
                parts = [array[g * group + i, :, pl.ds(128 * t, 128)] for g in range(4)]
                for k in range(4):
                    a, b, c, d = (
                        pltpu.roll(part, (32 * (g - k)) % 128, 1) if g != k else part
                        for g, part in enumerate(parts)
                    )
                    chunks[4 * t + k, f * group + i] = jnp.where(
                        lane < 32, a, jnp.where(lane < 64, b, jnp.where(lane < 96, c, d))
                    )
        return 0

    lax.fori_loop(0, group, pack, 0, unroll=2)
    shot = lax.axis_index("shot")
    for m, out in enumerate(outs):
        out[...] = chunks[shot ^ m]


def sum_kernel(model, *rest):
    parts, out = rest[:-1], rest[-1]
    group = out.shape[1] // 4
    for i in range(group):
        sums = []
        for f in (0, 1):
            value = parts[0][f * group + i]
            for part in parts[1:]:
                value = value + part[f * group + i]
            sums.append(value)
        for g in range(4):
            x = g * group + i
            a, c = (pltpu.roll(v, (128 - 32 * g) % 128, 1) if g else v for v in sums)
            s, e, d = (model[k, x] for k in range(3))
            out[0, x] = (e * a + d * c)[:, 0:32]
            out[1, x] = (s * a)[:, 0:32]
            out[2, x] = (s * c)[:, 0:32]


def per_device(
    speed, epsilon, delta, tilt, perturbation, forward_prev, forward_now, adjoint_prev, adjoint_now,
    wavelet, source_cell, receiver_cells,
):
    nx, ny, nz = speed.shape
    whole = (nx, ny, nz)
    pad = pltpu.VMEM((nx + 4, ny, nz), F32)
    half_rows = (nx // 2, ny, nz)
    packed = (nx // 2, ny, 128)
    model = (speed, epsilon, delta)

    yup, ydn, xup, xdn, mine, slices = call(
        prepare_kernel,
        [half_rows, half_rows, (4, ny, nz), (4, ny, nz), packed, (3, nx, ny, 128)],
        (forward_now, adjoint_now, perturbation) + model,
        [pltpu.VMEM((3, nx, ny, 128), F32)],
        name="prepare",
    )

    def exchange(yup, ydn, xup, xdn):
        return cycle(yup, "gy", 1), cycle(ydn, "gy", -1), cycle(xup, "gx", 1), cycle(xdn, "gx", -1)

    partner = lax.ppermute(mine, "shot", [(i, i ^ 1) for i in range(8)])
    halo = exchange(yup, ydn, xup, xdn)
    pair = jnp.concatenate([mine, partner], axis=0)
    others = [
        lax.ppermute(pair, "shot", [(i, (i // 2 + k) % 4 * 2 + i % 2) for i in range(8)]) for k in (1, 2, 3)
    ]
    (counts,) = call(
        functools.partial(counts_kernel, size_y=ny * lax.axis_size("gy"), depth=nz),
        [whole],
        (receiver_cells,),
        name="counts",
    )
    u1, l1, hu0, vu0, hl0, vl0 = call(
        first_kernel,
        [whole] * 6,
        (wavelet, source_cell, forward_now, forward_prev, adjoint_now, adjoint_prev)
        + halo + model + (tilt,),
        [pad, pad],
        (0, 1),
        name="first",
    )
    q1, q2, b1, d1, yup, ydn, xup, xdn = call(
        born_kernel,
        [whole] * 4 + [whole] * 2 + [(8, ny, nz)] * 2,
        (pair, *others, u1, l1, hu0, vu0, hl0, vl0),
        [pltpu.VMEM((8, nx // 2, ny, 128), F32)],
        name="born",
    )
    halo = exchange(yup, ydn, xup, xdn)
    u2, b2, hu1, vu1, hb1, vb1, yup, ydn, xup, xdn = call(
        second_kernel,
        [whole] * 6 + [half_rows] * 2 + [(4, ny, nz)] * 2,
        (wavelet, source_cell, forward_now, u1, b1, q1, q2) + halo + model + (tilt,),
        [pad, pad],
        (0, 1),
        name="second",
    )
    halo2 = exchange(yup, ydn, xup, xdn)
    l2, d2, a1, c1 = call(
        adjoint_kernel,
        [whole] * 4,
        (adjoint_now, l1, d1, b1, q1, q2, counts, hu1, vu1, hb1, vb1, u2, b2) + halo + model + (tilt,),
        [pad, pad],
        name="adjoint",
    )
    terms = call(
        image_kernel,
        [packed] * 8,
        (u2, b2) + halo2 + (l2, d2, a1, c1),
        [pad, pad, pltpu.VMEM(whole, F32), pltpu.VMEM((8, nx // 2, ny, 128), F32)],
        name="image",
    )
    arrived = [terms[0]] + [
        lax.ppermute(terms[m], "shot", [(i, i ^ m) for i in range(8)]) for m in range(1, 8)
    ]
    (out,) = call(sum_kernel, [(3, nx, ny, nz // 8)], (slices, *arrived), name="sum")
    return out


def solution(mesh):
    placed = (
        P("gx", "gy", None),
        P("gx", "gy", None),
        P("gx", "gy", None),
        P("gx", "gy", None),
        P(None, "gx", "gy", "shot"),
        P("shot", "gx", "gy", None),
        P("shot", "gx", "gy", None),
        P("shot", "gx", "gy", None),
        P("shot", "gx", "gy", None),
        P("shot", None),
        P("shot"),
        P("shot", None),
    )
    return jax.shard_map(
        per_device,
        mesh=mesh,
        in_specs=placed,
        out_specs=P(None, "gx", "gy", "shot"),
        check_vma=False,
    )
```

```python
import functools

import jax
import jax.numpy as jnp
from jax import lax
from jax.experimental import pallas as pl
from jax.experimental.pallas import tpu as pltpu
from jax.sharding import PartitionSpec as P

F32 = jnp.float32
BF16 = jnp.bfloat16
GROUP = 16
LIMIT = 24 * 1024 * 1024

S0, S1, S2 = -2.5, 4.0 / 3.0, -1.0 / 12.0
D1, D2 = 2.0 / 3.0, -1.0 / 12.0


def call(kernel, outs, ins, scratch=(), smem=(), hbm=(), after=(), name=None):
    place = {**dict.fromkeys(smem, pltpu.SMEM), **dict.fromkeys(hbm, pltpu.HBM)}
    place |= {len(ins) + i: pl.ANY for i in range(len(after))}
    ins = (*ins, *after)
    typed = [out if out[-1] is BF16 else (out, F32) for out in outs]
    return pl.pallas_call(
        kernel,
        out_shape=[jax.ShapeDtypeStruct(*out) for out in typed],
        in_specs=[pl.BlockSpec(memory_space=place.get(i, pltpu.VMEM)) for i in range(len(ins))],
        out_specs=[pl.BlockSpec(memory_space=pltpu.VMEM)] * len(outs),
        scratch_shapes=list(scratch),
        compiler_params=pltpu.CompilerParams(vmem_limit_bytes=LIMIT),
        name=name,
    )(*ins)


def cycle(value, axis, step):
    size = lax.axis_size(axis)
    return lax.ppermute(value, axis, [(i, (i + step) % size) for i in range(size)])


def across(value):
    return lax.ppermute(value, "shot", [(i, i ^ 1) for i in range(8)])


def along(value, step):
    return lax.ppermute(value, "shot", [(i, (i // 2 + step) % 4 * 2 + i % 2) for i in range(8)])


def rows():
    return lax.broadcasted_iota(jnp.int32, (8, 128), 0)


def lanes():
    return lax.broadcasted_iota(jnp.int32, (8, 128), 1)


def pack_y(fields, up, down):
    row = rows()
    nx = fields[0].shape[0]
    for i in range(nx // 2):
        for h in (0, 128):
            tile = pl.ds(h, 128)
            for out, base in ((up, 6), (down, 0)):
                acc = None
                for piece in (0, 1):
                    for f, field in enumerate(fields):
                        at = 4 * piece + 2 * f
                        value = field[i + piece * (nx // 2), :, tile]
                        value = pltpu.roll(value, (at - base) % 8, 0) if at != base else value
                        acc = value if acc is None else jnp.where(row >= at, value, acc)
                out[i, :, tile] = acc


def pack_x(fields, up, down):
    for f, field in enumerate(fields):
        n = field.shape[0]
        up[2 * f : 2 * f + 2] = field[n - 2 : n]
        down[2 * f : 2 * f + 2] = field[0:2]


def fill(pad, field, before, after, f):
    n = field.shape[0]
    gx = lax.axis_index("gx")
    pad[2 : n + 2] = field[...]
    pad[0:2] = jnp.where(gx > 0, before[2 * f : 2 * f + 2], 0.0)
    pad[n + 2 : n + 4] = jnp.where(gx < lax.axis_size("gx") - 1, after[2 * f : 2 * f + 2], 0.0)


def edge_rows(before, after, x, f, half):
    row = rows()
    gy = lax.axis_index("gy")
    first, last = gy > 0, gy < lax.axis_size("gy") - 1
    i, at = x % half, 4 * (x // half) + 2 * f
    out = []
    for t in (0, 1):
        tile = pl.ds(128 * t, 128)
        lower, upper = before[i, :, tile], after[i, :, tile]
        lower = pltpu.roll(lower, (6 - at) % 8, 0) if at != 6 else lower
        upper = pltpu.roll(upper, (-at) % 8, 0) if at != 0 else upper
        out.append(jnp.where((row >= 6) & first, lower, jnp.where((row <= 1) & last, upper, 0.0)))
    return out


def along_z(values, matrix):
    total = None
    for _ in range(3):
        part = values.astype(BF16)
        values = values - part.astype(F32)
        term = jnp.dot(part, matrix, preferred_element_type=F32)
        total = term if total is None else total + term
    return total * (1.0 / 12.0)


def lateral(pad, x, edge, slope=True):
    row = rows()
    horizontal, slopes, centre = [], [], []
    for t in (0, 1):
        tile = pl.ds(128 * t, 128)
        c = pad[x + 2, :, tile]
        xl, xh, xl2, xh2 = (pad[x + k, :, tile] for k in (1, 3, 0, 4))
        e = edge[t]
        yl = pltpu.roll(jnp.where(row == 7, e, c), 1, 0)
        yl2 = pltpu.roll(jnp.where(row >= 6, e, c), 2, 0)
        yh = pltpu.roll(jnp.where(row == 0, e, c), 7, 0)
        yh2 = pltpu.roll(jnp.where(row <= 1, e, c), 6, 0)
        horizontal.append(2.0 * S0 * c + S1 * ((xl + xh) + (yl + yh)) + S2 * ((xl2 + xh2) + (yl2 + yh2)))
        if slope:
            slopes.append(D1 * ((xh - xl) + (yh - yl)) + D2 * ((xh2 - xl2) + (yh2 - yl2)))
        centre.append(c)
    return horizontal, slopes, centre


def slabs(lists):
    return jnp.concatenate([jnp.concatenate(pair, axis=1) for pair in lists], axis=0)


def derivs(pad, before, after, f, zmat, emit):
    nx = pad.shape[0] - 4
    for at in range(0, nx, GROUP):
        found = [lateral(pad, x, edge_rows(before, after, x, f, nx // 2)) for x in range(at, at + GROUP)]
        vertical = along_z(slabs([c for _, _, c in found]), zmat[0])
        mixed = along_z(slabs([s for _, s, _ in found]), zmat[1])
        for j, (horizontal, _, centre) in enumerate(found):
            for t in (0, 1):
                part = (slice(8 * j, 8 * j + 8), slice(128 * t, 128 * t + 128))
                emit(at + j, t, horizontal[t], vertical[part], mixed[part], centre[t])


def second_z(field, zmat, emit):
    for at in range(0, field.shape[0], GROUP):
        vertical = along_z(field[at : at + GROUP].reshape(GROUP * 8, field.shape[2]), zmat[0])
        for j in range(GROUP):
            for t in (0, 1):
                emit(at + j, t, vertical[8 * j : 8 * j + 8, 128 * t : 128 * t + 128])


def operate(model, x, tile, h, v, m):
    s, e, d, k = (w[x, :, tile] for w in model)
    return s * (e * h + d * v) + k * m


def chunk_kernel(p, speed, epsilon, delta, chunk, model, zmat, pbuf, half, sems):
    shot = lax.axis_index("shot")
    lower = pl.ds(pl.multiple_of((shot // 4) * 128, 128), 128)
    copies = [
        pltpu.make_async_copy(array.at[:, :, lower], half.at[k], sems.at[k])
        for k, array in enumerate((speed, epsilon, delta))
    ]
    for copy in copies:
        copy.start()
    depth = zmat.shape[1]
    offset = lax.broadcasted_iota(jnp.int32, (depth, depth), 0) - lax.broadcasted_iota(
        jnp.int32, (depth, depth), 1
    )
    far = jnp.abs(offset)
    second = jnp.where(far == 0, -30.0, jnp.where(far == 1, 16.0, jnp.where(far == 2, -1.0, 0.0)))
    first = jnp.where(far == 1, 8.0, jnp.where(far == 2, -1.0, 0.0))
    zmat[0] = second.astype(BF16)
    zmat[1] = jnp.where(offset > 0, first, -first).astype(BF16)
    pbuf[:, :, :, 0:32] = p[...]
    for copy in copies:
        copy.wait()
    shift = lax.rem(128 - 32 * lax.rem(shot, 4), 128)
    lane = lanes()
    group = p.shape[1] // 4
    for i in range(group):
        parts = [[], []]
        for g in range(4):
            x = g * group + i
            p0, p1, p2 = (pbuf[k, x] for k in range(3))
            s, e, d = (pltpu.roll(half[k, x], shift, 1) for k in range(3))
            for k, w in enumerate((s, e, d)):
                model[k, x] = w
            for f, q in enumerate((p0 * e + s * p1, p0 * d + s * p2)):
                parts[f].append(pltpu.roll(q, 32 * g, 1) if g else q)
        for f in (0, 1):
            a, b, c, d = parts[f]
            chunk[f * group + i] = jnp.where(
                lane < 32, a, jnp.where(lane < 64, b, jnp.where(lane < 96, c, d))
            )


def y_kernel(a, b, *rest):
    pack_y([a, b], *rest[-2:])


def x_kernel(a, b, *rest):
    pack_x([a, b], *rest[-2:])


def first_kernel(
    wavelet, source, zmat, u, um, l, lm, ylo, yhi, xlo, xhi, speed, epsilon, delta, tilt,
    u1, l1, hu, vu, hl, vl, padu, padl,
):
    model = (speed, epsilon, delta, tilt)
    lane = lanes()
    amount, depth = wavelet[0, 0], source[0]
    for f, (pad, w, prev, new, h_out, v_out) in enumerate(
        ((padu, u, um, u1, hu, vu), (padl, l, lm, l1, hl, vl))
    ):
        fill(pad, w.at[0], xlo, xhi, f)

        def emit(x, t, h, v, m, c, f=f, prev=prev, new=new, h_out=h_out, v_out=v_out):
            tile = pl.ds(128 * t, 128)
            h_out[x, :, tile] = h
            v_out[x, :, tile] = v
            value = 2.0 * c - prev[0, x, :, tile] + operate(model, x, tile, h, v, m)
            if f == 0:
                value = value + jnp.where(lane + 128 * t == depth, amount, 0.0)
            new[x, :, tile] = value

        derivs(pad, ylo, yhi, f, zmat, emit)


def born_kernel(
    mine, partner, before, behind, opposite, beside, u1, l1, hu, vu, hl, vl, q1, q2, b1, d1, yup, ydn, xup, xdn, chunks,
):
    shot = lax.axis_index("shot")
    y, xh = shot // 2, lax.rem(shot, 2)
    group = hu.shape[0] // 4
    n = 2 * group
    for k, same, other in (
        (0, mine[...], partner[...]),
        (3, before[...], beside[0:n]),
        (1, behind[...], beside[n : 2 * n]),
        (2, opposite[0:n], opposite[n : 2 * n]),
    ):
        there = lax.rem(y + k, 4) * 2
        chunks[there + xh] = same
        chunks[there + 1 - xh] = other
    lane = lanes()
    for x in range(4 * group):
        g, i = x // group, x % group
        for t in (0, 1):
            tile = pl.ds(128 * t, 128)
            both = []
            for f in (0, 1):
                parts = []
                for k in range(4):
                    part = chunks[4 * t + k, f * group + i]
                    parts.append(pltpu.roll(part, (32 * (k - g)) % 128, 1) if k != g else part)
                a, b, c, d = parts
                both.append(jnp.where(lane < 32, a, jnp.where(lane < 64, b, jnp.where(lane < 96, c, d))))
            q1[x, :, tile], q2[x, :, tile] = both
            b1[x, :, tile] = both[0] * hu[x, :, tile] + both[1] * vu[x, :, tile]
            d1[x, :, tile] = both[0] * hl[x, :, tile] + both[1] * vl[x, :, tile]
    pack_y([u1, b1], yup, ydn)
    pack_x([u1, b1, l1, d1], xup, xdn)


def second_kernel(
    wavelet, source, zmat, u, u1, b1, q1, q2, ylo, yhi, xlo, xhi, speed, epsilon, delta, tilt,
    u2, b2, hu, vu, hb, vb, yup, ydn, xup, xdn, padu, padb,
):
    model = (speed, epsilon, delta, tilt)
    lane = lanes()
    amount, depth = wavelet[0, 1], source[0]
    fill(padu, u1, xlo, xhi, 0)
    fill(padb, b1, xlo, xhi, 1)

    def emit_u(x, t, h, v, m, c):
        tile = pl.ds(128 * t, 128)
        hu[x, :, tile] = h
        vu[x, :, tile] = v
        u2[x, :, tile] = (
            2.0 * c - u[0, x, :, tile] + operate(model, x, tile, h, v, m)
            + jnp.where(lane + 128 * t == depth, amount, 0.0)
        )

    def emit_b(x, t, h, v, m, c):
        tile = pl.ds(128 * t, 128)
        hb[x, :, tile] = h
        vb[x, :, tile] = v
        b2[x, :, tile] = (
            2.0 * c + operate(model, x, tile, h, v, m)
            + (q1[x, :, tile] * hu[x, :, tile] + q2[x, :, tile] * vu[x, :, tile])
        )

    derivs(padu, ylo, yhi, 0, zmat, emit_u)
    derivs(padb, ylo, yhi, 1, zmat, emit_b)
    fields = [u2, b2]
    pack_y(fields, yup, ydn)
    pack_x(fields, xup, xdn)


def counts_kernel(cells, out, *, size_y, depth):
    nx, ny = out.shape[0], out.shape[1]
    gx, gy = lax.axis_index("gx"), lax.axis_index("gy")
    index = cells[...]
    cx = lax.div(index, size_y * depth) - gx * nx
    cy = lax.rem(lax.div(index, depth), size_y) - gy * ny
    cz = lax.rem(index, depth)
    inside = (cx >= 0) & (cx < nx) & (cy >= 0) & (cy < ny)
    place = jnp.where(inside, cx * ny + cy, -1)
    n = index.shape[1]
    left = jnp.where(lax.broadcasted_iota(jnp.int32, (nx * ny, n), 0) == place, 1.0, 0.0).astype(BF16)
    right = jnp.where(lax.broadcasted_iota(jnp.int32, (depth, n), 0) == cz, 1.0, 0.0).astype(BF16)
    total = lax.dot_general(left, right, (((1,), (1,)), ((), ())), preferred_element_type=F32)
    out[...] = total.reshape(nx, ny, depth)


def adjoint_kernel(
    zmat, l, l1, d1, b1, q1, q2, counts, hu, vu, hb, vb, u2, b2, ylo, yhi, xlo, xhi,
    speed, epsilon, delta, tilt, l2, d2, a1, c1, padl, padd, hl, vl,
):
    model = (speed, epsilon, delta, tilt)
    fill(padl, l1, xlo, xhi, 2)
    fill(padd, d1, xlo, xhi, 3)

    def emit_l(x, t, h, v, m, c):
        tile = pl.ds(128 * t, 128)
        hl[x, :, tile] = h
        vl[x, :, tile] = v
        l2[x, :, tile] = 2.0 * c - l[0, x, :, tile] + operate(model, x, tile, h, v, m)

    def emit_d(x, t, h, v, m, c):
        tile = pl.ds(128 * t, 128)
        d2[x, :, tile] = (
            2.0 * c + operate(model, x, tile, h, v, m)
            + (q1[x, :, tile] * hl[x, :, tile] + q2[x, :, tile] * vl[x, :, tile])
            + counts[x, :, tile] * b1[x, :, tile]
        )
        a1[x, :, tile] = hu[x, :, tile] * c + hb[x, :, tile] * l1[x, :, tile]
        c1[x, :, tile] = vu[x, :, tile] * c + vb[x, :, tile] * l1[x, :, tile]

    derivs(padl, ylo, yhi, 0, zmat, emit_l)
    derivs(padd, ylo, yhi, 1, zmat, emit_d)

    for field, other in ((u2, d2), (b2, l2)):

        def add(x, t, v, other=other):
            tile = pl.ds(128 * t, 128)
            c1[x, :, tile] = c1[x, :, tile] + v * other[x, :, tile]

        second_z(field, zmat, add)


def image_kernel(
    u2, b2, ylo, yhi, xlo, xhi, l2, d2, a1, c1, keep, opposite, beside, padu, padb, total, chunks,
):
    for f, (pad, w) in enumerate(((padu, u2), (padb, b2))):
        fill(pad, w, xlo, xhi, f)
    nx = u2.shape[0]
    for x in range(nx):
        hu, hb = (
            lateral(pad, x, edge_rows(ylo, yhi, x, f, nx // 2), False)[0] for f, pad in enumerate((padu, padb))
        )
        for t in (0, 1):
            tile = pl.ds(128 * t, 128)
            total[x, :, tile] = a1[x, :, tile] + hu[t] * d2[x, :, tile] + hb[t] * l2[x, :, tile]
    lane = lanes()
    group = nx // 4
    for i in range(group):
        for f, array in enumerate((total, c1)):
            for t in (0, 1):
                parts = [array[g * group + i, :, pl.ds(128 * t, 128)] for g in range(4)]
                for k in range(4):
                    a, b, c, d = (
                        pltpu.roll(part, (32 * (g - k)) % 128, 1) if g != k else part
                        for g, part in enumerate(parts)
                    )
                    chunks[4 * t + k, f * group + i] = jnp.where(
                        lane < 32, a, jnp.where(lane < 64, b, jnp.where(lane < 96, c, d))
                    )
    shot = lax.axis_index("shot")
    y, xh = shot // 2, lax.rem(shot, 2)

    def chunk_at(step, same):
        return chunks[lax.rem(y + step, 4) * 2 + (xh if same else 1 - xh)]

    for out, wanted in (
        (keep, ((0, True), (0, False), (1, True), (3, True))),
        (opposite, ((2, True), (2, False))),
        (beside, ((1, False), (3, False))),
    ):
        for i, (step, same) in enumerate(wanted):
            out[i] = chunk_at(step, same)


def merge_kernel(keep, opposite, beside, own, other, up, down):
    own[...] = keep[0] + opposite[0]
    other[...] = keep[1] + opposite[1]
    up[...] = keep[2] + beside[0]
    down[...] = keep[3] + beside[1]


def sum_kernel(model, own, other, up, down, out):
    group = out.shape[1] // 4
    for i in range(group):
        sums = []
        for f in (0, 1):
            j = f * group + i
            sums.append((own[j] + other[j]) + (up[j] + down[j]))
        for g in range(4):
            x = g * group + i
            a, c = (pltpu.roll(v, (128 - 32 * g) % 128, 1) if g else v for v in sums)
            s, e, d = (model[k, x] for k in range(3))
            out[0, x] = (e * a + d * c)[:, 0:32]
            out[1, x] = (s * a)[:, 0:32]
            out[2, x] = (s * c)[:, 0:32]


def per_device(
    speed, epsilon, delta, tilt, perturbation, forward_prev, forward_now, adjoint_prev, adjoint_now,
    wavelet, source_cell, receiver_cells,
):
    nx, ny, nz = speed.shape
    whole = (nx, ny, nz)
    pad = pltpu.VMEM((nx + 4, ny, nz), F32)
    half_rows = (nx // 2, ny, nz)
    layers = [half_rows] * 2 + [(4, ny, nz)] * 2
    packed = (nx // 2, ny, 128)
    model = (speed, epsilon, delta, tilt)

    def exchange_y(up, down):
        return cycle(up, "gy", 1), cycle(down, "gy", -1)

    def exchange_x(up, down):
        return cycle(up, "gx", 1), cycle(down, "gx", -1)

    mine, slices, zmat = call(
        chunk_kernel,
        [packed, (3, nx, ny, 128), ((2, nz, nz), BF16)],
        (perturbation, speed, epsilon, delta),
        [pltpu.VMEM((3, nx, ny, 128), F32), pltpu.VMEM((3, nx, ny, 128), F32), pltpu.SemaphoreType.DMA((3,))],
        hbm=(1, 2, 3),
        name="chunk",
    )
    partner, before, behind = across(mine), along(mine, 1), along(mine, -1)
    now = (forward_now[0], adjoint_now[0])
    y0 = exchange_y(*call(y_kernel, layers[:2], now, after=(mine,), name="layers_y"))
    opposite = along(jnp.concatenate([mine, partner], axis=0), 2)
    beside = across(jnp.concatenate([before, behind], axis=0))
    x0 = exchange_x(*call(x_kernel, layers[2:], now, after=y0, name="layers_x"))
    (counts,) = call(
        functools.partial(counts_kernel, size_y=ny * lax.axis_size("gy"), depth=nz),
        [whole],
        (receiver_cells,),
        name="counts",
    )
    u1, l1, hu0, vu0, hl0, vl0 = call(
        first_kernel,
        [whole] * 6,
        (wavelet, source_cell, zmat, forward_now, forward_prev, adjoint_now, adjoint_prev) + y0 + x0 + model,
        [pad, pad],
        (0, 1),
        name="first",
    )
    q1, q2, b1, d1, yup, ydn, xup, xdn = call(
        born_kernel,
        [whole] * 4 + layers[:2] + [(8, ny, nz)] * 2,
        (mine, partner, before, behind, opposite, beside, u1, l1, hu0, vu0, hl0, vl0),
        [pltpu.VMEM((8, nx // 2, ny, 128), F32)],
        name="born",
    )
    y_ub = exchange_y(yup, ydn)
    x1 = exchange_x(xup, xdn)
    y_ld = exchange_y(*call(y_kernel, layers[:2], (l1, d1), name="adjoint_y"))
    u2, b2, hu1, vu1, hb1, vb1, yup, ydn, xup, xdn = call(
        second_kernel,
        [whole] * 6 + layers,
        (wavelet, source_cell, zmat, forward_now, u1, b1, q1, q2) + y_ub + x1 + model,
        [pad, pad],
        (0, 1),
        name="second",
    )
    halo = exchange_y(yup, ydn) + exchange_x(xup, xdn)
    l2, d2, a1, c1 = call(
        adjoint_kernel,
        [whole] * 4,
        (zmat, adjoint_now, l1, d1, b1, q1, q2, counts, hu1, vu1, hb1, vb1, u2, b2) + y_ld + x1 + model,
        [pad, pad, pltpu.VMEM(whole, F32), pltpu.VMEM(whole, F32)],
        name="adjoint",
    )
    keep, opposite, beside = call(
        image_kernel,
        [(4,) + packed, (2,) + packed, (2,) + packed],
        (u2, b2) + halo + (l2, d2, a1, c1),
        [pad, pad, pltpu.VMEM(whole, F32), pltpu.VMEM((8,) + packed, F32)],
        name="image",
    )
    own, other, up, down = call(
        merge_kernel, [packed] * 4, (keep, along(opposite, 2), across(beside)), name="merge"
    )
    (out,) = call(
        sum_kernel,
        [(3, nx, ny, nz // 8)],
        (slices, own, across(other), along(up, 1), along(down, -1)),
        name="sum",
    )
    return out


def solution(mesh):
    placed = (
        P("gx", "gy", None),
        P("gx", "gy", None),
        P("gx", "gy", None),
        P("gx", "gy", None),
        P(None, "gx", "gy", "shot"),
        P("shot", "gx", "gy", None),
        P("shot", "gx", "gy", None),
        P("shot", "gx", "gy", None),
        P("shot", "gx", "gy", None),
        P("shot", None),
        P("shot"),
        P("shot", None),
    )
    return jax.shard_map(
        per_device,
        mesh=mesh,
        in_specs=placed,
        out_specs=P(None, "gx", "gy", "shot"),
        check_vma=False,
    )
```

```python
import functools

import jax
import jax.numpy as jnp
from jax import lax
from jax.experimental import pallas as pl
from jax.experimental.pallas import tpu as pltpu
from jax.sharding import PartitionSpec as P

F32 = jnp.float32
BF16 = jnp.bfloat16
GROUP = 16
LIMIT = 24 * 1024 * 1024

S0, S1, S2 = -2.5, 4.0 / 3.0, -1.0 / 12.0
D1, D2 = 2.0 / 3.0, -1.0 / 12.0


def call(kernel, outs, ins, scratch=(), smem=(), hbm=(), after=(), name=None):
    place = {**dict.fromkeys(smem, pltpu.SMEM), **dict.fromkeys(hbm, pltpu.HBM)}
    place |= {len(ins) + i: pl.ANY for i in range(len(after))}
    ins = (*ins, *after)
    typed = [out if out[-1] is BF16 else (out, F32) for out in outs]
    return pl.pallas_call(
        kernel,
        out_shape=[jax.ShapeDtypeStruct(*out) for out in typed],
        in_specs=[pl.BlockSpec(memory_space=place.get(i, pltpu.VMEM)) for i in range(len(ins))],
        out_specs=[pl.BlockSpec(memory_space=pltpu.VMEM)] * len(outs),
        scratch_shapes=list(scratch),
        compiler_params=pltpu.CompilerParams(vmem_limit_bytes=LIMIT),
        name=name,
    )(*ins)


def cycle(value, axis, step):
    size = lax.axis_size(axis)
    return lax.ppermute(value, axis, [(i, (i + step) % size) for i in range(size)])


def across(value):
    return lax.ppermute(value, "shot", [(i, i ^ 1) for i in range(8)])


def along(value, step):
    return lax.ppermute(value, "shot", [(i, (i // 2 + step) % 4 * 2 + i % 2) for i in range(8)])


def rows():
    return lax.broadcasted_iota(jnp.int32, (8, 128), 0)


def lanes():
    return lax.broadcasted_iota(jnp.int32, (8, 128), 1)


def pack_y(fields, up, down):
    row = rows()
    nx = fields[0].shape[0]
    for i in range(nx // 2):
        for h in (0, 128):
            tile = pl.ds(h, 128)
            for out, base in ((up, 6), (down, 0)):
                acc = None
                for piece in (0, 1):
                    for f, field in enumerate(fields):
                        at = 4 * piece + 2 * f
                        value = field[i + piece * (nx // 2), :, tile]
                        value = pltpu.roll(value, (at - base) % 8, 0) if at != base else value
                        acc = value if acc is None else jnp.where(row >= at, value, acc)
                out[i, :, tile] = acc


def even_x():
    return lax.rem(lax.axis_index("gx"), 2) == 0


def face_x(first, last, inner, outer, f):
    even = even_x()
    inner[2 * f : 2 * f + 2] = jnp.where(even, last, first)
    outer[2 * f : 2 * f + 2] = jnp.where(even, first, last)


def pack_x(fields, inner, outer):
    for f, field in enumerate(fields):
        n = field.shape[0]
        face_x(field[0:2], field[n - 2 : n], inner, outer, f)


def fill(pad, field, inner, outer, f):
    n = field.shape[0]
    gx, even = lax.axis_index("gx"), even_x()
    inner, outer = inner[2 * f : 2 * f + 2], outer[2 * f : 2 * f + 2]
    pad[2 : n + 2] = field[...]
    pad[0:2] = jnp.where(gx > 0, jnp.where(even, outer, inner), 0.0)
    pad[n + 2 : n + 4] = jnp.where(gx < lax.axis_size("gx") - 1, jnp.where(even, inner, outer), 0.0)


def edge_rows(before, after, x, f, half):
    row = rows()
    gy = lax.axis_index("gy")
    first, last = gy > 0, gy < lax.axis_size("gy") - 1
    i, at = x % half, 4 * (x // half) + 2 * f
    out = []
    for t in (0, 1):
        tile = pl.ds(128 * t, 128)
        lower, upper = before[i, :, tile], after[i, :, tile]
        lower = pltpu.roll(lower, (6 - at) % 8, 0) if at != 6 else lower
        upper = pltpu.roll(upper, (-at) % 8, 0) if at != 0 else upper
        out.append(jnp.where((row >= 6) & first, lower, jnp.where((row <= 1) & last, upper, 0.0)))
    return out


def along_z(values, matrix):
    total = None
    for _ in range(3):
        part = values.astype(BF16)
        values = values - part.astype(F32)
        term = jnp.dot(part, matrix, preferred_element_type=F32)
        total = term if total is None else total + term
    return total * (1.0 / 12.0)


def lateral(pad, x, edge, slope=True):
    row = rows()
    horizontal, slopes, centre = [], [], []
    for t in (0, 1):
        tile = pl.ds(128 * t, 128)
        c = pad[x + 2, :, tile]
        xl, xh, xl2, xh2 = (pad[x + k, :, tile] for k in (1, 3, 0, 4))
        e = edge[t]
        yl = pltpu.roll(jnp.where(row == 7, e, c), 1, 0)
        yl2 = pltpu.roll(jnp.where(row >= 6, e, c), 2, 0)
        yh = pltpu.roll(jnp.where(row == 0, e, c), 7, 0)
        yh2 = pltpu.roll(jnp.where(row <= 1, e, c), 6, 0)
        horizontal.append(2.0 * S0 * c + S1 * ((xl + xh) + (yl + yh)) + S2 * ((xl2 + xh2) + (yl2 + yh2)))
        if slope:
            slopes.append(D1 * ((xh - xl) + (yh - yl)) + D2 * ((xh2 - xl2) + (yh2 - yl2)))
        centre.append(c)
    return horizontal, slopes, centre


def slabs(lists):
    return jnp.concatenate([jnp.concatenate(pair, axis=1) for pair in lists], axis=0)


def derivs(pad, before, after, f, zmat, emit):
    nx = pad.shape[0] - 4
    for at in range(0, nx, GROUP):
        found = [lateral(pad, x, edge_rows(before, after, x, f, nx // 2)) for x in range(at, at + GROUP)]
        vertical = along_z(slabs([c for _, _, c in found]), zmat[0])
        mixed = along_z(slabs([s for _, s, _ in found]), zmat[1])
        for j, (horizontal, _, centre) in enumerate(found):
            for t in (0, 1):
                part = (slice(8 * j, 8 * j + 8), slice(128 * t, 128 * t + 128))
                emit(at + j, t, horizontal[t], vertical[part], mixed[part], centre[t])


def second_z(field, zmat, emit):
    for at in range(0, field.shape[0], GROUP):
        vertical = along_z(field[at : at + GROUP].reshape(GROUP * 8, field.shape[2]), zmat[0])
        for j in range(GROUP):
            for t in (0, 1):
                emit(at + j, t, vertical[8 * j : 8 * j + 8, 128 * t : 128 * t + 128])


def operate(model, x, tile, h, v, m):
    s, e, d, k = (w[x, :, tile] for w in model)
    return s * (e * h + d * v) + k * m


def z_matrices(out):
    shape = out.shape[1:]
    offset = lax.broadcasted_iota(jnp.int32, shape, 0) - lax.broadcasted_iota(jnp.int32, shape, 1)
    far = jnp.abs(offset)
    second = jnp.where(far == 0, -30.0, jnp.where(far == 1, 16.0, jnp.where(far == 2, -1.0, 0.0)))
    first = jnp.where(far == 1, 8.0, jnp.where(far == 2, -1.0, 0.0))
    out[0] = second.astype(BF16)
    out[1] = jnp.where(offset > 0, first, -first).astype(BF16)


def own_depth(shot):
    tile = pl.ds(pl.multiple_of((shot // 4) * 128, 128), 128)
    return tile, lax.rem(128 - 32 * lax.rem(shot, 4), 128)


def chunk_kernel(p, speed, epsilon, delta, *rest):
    chunk, pbuf = rest[-2:]
    pbuf[:, :, :, 0:32] = p[...]
    tile, shift = own_depth(lax.axis_index("shot"))
    lane = lanes()
    group = p.shape[1] // 4
    for i in range(group):
        parts = [[], []]
        for g in range(4):
            x = g * group + i
            p0, p1, p2 = (pbuf[k, x] for k in range(3))
            s, e, d = (pltpu.roll(w[x, :, tile], shift, 1) for w in (speed, epsilon, delta))
            for f, q in enumerate((p0 * e + s * p1, p0 * d + s * p2)):
                parts[f].append(pltpu.roll(q, 32 * g, 1) if g else q)
        for f in (0, 1):
            a, b, c, d = parts[f]
            chunk[f * group + i] = jnp.where(
                lane < 32, a, jnp.where(lane < 64, b, jnp.where(lane < 96, c, d))
            )


def first_x_kernel(u_first, l_first, u_last, l_last, inner, outer):
    for f, (first, last) in enumerate(((u_first, u_last), (l_first, l_last))):
        face_x(first[0:2], last[6:8], inner, outer, f)


def first_y_kernel(u, l, *rest):
    up, down, zmat = rest[-3:]
    pack_y([u, l], up, down)
    z_matrices(zmat)


def y_kernel(a, b, up, down):
    pack_y([a, b], up, down)


def first_kernel(
    wavelet, source, zmat, u, um, l, lm, ylo, yhi, inner, outer, speed, epsilon, delta, tilt, _,
    u1, l1, hu, vu, hl, vl, padu, padl,
):
    model = (speed, epsilon, delta, tilt)
    lane = lanes()
    amount, depth = wavelet[0, 0], source[0]
    for f, (pad, w, prev, new, h_out, v_out) in enumerate(
        ((padu, u, um, u1, hu, vu), (padl, l, lm, l1, hl, vl))
    ):
        fill(pad, w.at[0], inner, outer, f)

        def emit(x, t, h, v, m, c, f=f, prev=prev, new=new, h_out=h_out, v_out=v_out):
            tile = pl.ds(128 * t, 128)
            h_out[x, :, tile] = h
            v_out[x, :, tile] = v
            value = 2.0 * c - prev[0, x, :, tile] + operate(model, x, tile, h, v, m)
            if f == 0:
                value = value + jnp.where(lane + 128 * t == depth, amount, 0.0)
            new[x, :, tile] = value

        derivs(pad, ylo, yhi, f, zmat, emit)


def born_kernel(
    mine, partner, before, behind, opposite, beside, u1, l1, hu, vu, hl, vl, q1, q2, b1, d1, yup, ydn, inner_out, outer_out, chunks,
):
    shot = lax.axis_index("shot")
    y, xh = shot // 2, lax.rem(shot, 2)
    group = hu.shape[0] // 4
    n = 2 * group
    for k, same, other in (
        (0, mine[...], partner[...]),
        (3, before[...], beside[0:n]),
        (1, behind[...], beside[n : 2 * n]),
        (2, opposite[0:n], opposite[n : 2 * n]),
    ):
        there = lax.rem(y + k, 4) * 2
        chunks[there + xh] = same
        chunks[there + 1 - xh] = other
    lane = lanes()
    for x in range(4 * group):
        g, i = x // group, x % group
        for t in (0, 1):
            tile = pl.ds(128 * t, 128)
            both = []
            for f in (0, 1):
                parts = []
                for k in range(4):
                    part = chunks[4 * t + k, f * group + i]
                    parts.append(pltpu.roll(part, (32 * (k - g)) % 128, 1) if k != g else part)
                a, b, c, d = parts
                both.append(jnp.where(lane < 32, a, jnp.where(lane < 64, b, jnp.where(lane < 96, c, d))))
            q1[x, :, tile], q2[x, :, tile] = both
            b1[x, :, tile] = both[0] * hu[x, :, tile] + both[1] * vu[x, :, tile]
            d1[x, :, tile] = both[0] * hl[x, :, tile] + both[1] * vl[x, :, tile]
    pack_y([u1, b1], yup, ydn)
    pack_x([u1, b1, l1, d1], inner_out, outer_out)


def second_kernel(
    wavelet, source, zmat, u, u1, b1, q1, q2, ylo, yhi, inner, outer, speed, epsilon, delta, tilt,
    u2, b2, hu, vu, hb, vb, yup, ydn, inner_out, outer_out, padu, padb,
):
    model = (speed, epsilon, delta, tilt)
    lane = lanes()
    amount, depth = wavelet[0, 1], source[0]
    fill(padu, u1, inner, outer, 0)
    fill(padb, b1, inner, outer, 1)

    def emit_u(x, t, h, v, m, c):
        tile = pl.ds(128 * t, 128)
        hu[x, :, tile] = h
        vu[x, :, tile] = v
        u2[x, :, tile] = (
            2.0 * c - u[0, x, :, tile] + operate(model, x, tile, h, v, m)
            + jnp.where(lane + 128 * t == depth, amount, 0.0)
        )

    def emit_b(x, t, h, v, m, c):
        tile = pl.ds(128 * t, 128)
        hb[x, :, tile] = h
        vb[x, :, tile] = v
        b2[x, :, tile] = (
            2.0 * c + operate(model, x, tile, h, v, m)
            + (q1[x, :, tile] * hu[x, :, tile] + q2[x, :, tile] * vu[x, :, tile])
        )

    derivs(padu, ylo, yhi, 0, zmat, emit_u)
    derivs(padb, ylo, yhi, 1, zmat, emit_b)
    fields = [u2, b2]
    pack_y(fields, yup, ydn)
    pack_x(fields, inner_out, outer_out)


def counts_kernel(cells, *rest, size_y, depth):
    out = rest[-1]
    nx, ny = out.shape[0], out.shape[1]
    gx, gy = lax.axis_index("gx"), lax.axis_index("gy")
    index = cells[...]
    cx = lax.div(index, size_y * depth) - gx * nx
    cy = lax.rem(lax.div(index, depth), size_y) - gy * ny
    cz = lax.rem(index, depth)
    inside = (cx >= 0) & (cx < nx) & (cy >= 0) & (cy < ny)
    place = jnp.where(inside, cx * ny + cy, -1)
    n = index.shape[1]
    left = jnp.where(lax.broadcasted_iota(jnp.int32, (nx * ny, n), 0) == place, 1.0, 0.0).astype(BF16)
    right = jnp.where(lax.broadcasted_iota(jnp.int32, (depth, n), 0) == cz, 1.0, 0.0).astype(BF16)
    total = lax.dot_general(left, right, (((1,), (1,)), ((), ())), preferred_element_type=F32)
    out[...] = total.reshape(nx, ny, depth)


def adjoint_kernel(
    zmat, l, l1, d1, b1, q1, q2, counts, hu, vu, hb, vb, u2, b2, ylo, yhi, inner, outer,
    speed, epsilon, delta, tilt, l2, d2, a1, c1, padl, padd, hl, vl,
):
    model = (speed, epsilon, delta, tilt)
    fill(padl, l1, inner, outer, 2)
    fill(padd, d1, inner, outer, 3)

    def emit_l(x, t, h, v, m, c):
        tile = pl.ds(128 * t, 128)
        hl[x, :, tile] = h
        vl[x, :, tile] = v
        l2[x, :, tile] = 2.0 * c - l[0, x, :, tile] + operate(model, x, tile, h, v, m)

    def emit_d(x, t, h, v, m, c):
        tile = pl.ds(128 * t, 128)
        d2[x, :, tile] = (
            2.0 * c + operate(model, x, tile, h, v, m)
            + (q1[x, :, tile] * hl[x, :, tile] + q2[x, :, tile] * vl[x, :, tile])
            + counts[x, :, tile] * b1[x, :, tile]
        )
        a1[x, :, tile] = hu[x, :, tile] * c + hb[x, :, tile] * l1[x, :, tile]
        c1[x, :, tile] = vu[x, :, tile] * c + vb[x, :, tile] * l1[x, :, tile]

    derivs(padl, ylo, yhi, 0, zmat, emit_l)
    derivs(padd, ylo, yhi, 1, zmat, emit_d)

    for field, other in ((u2, d2), (b2, l2)):

        def add(x, t, v, other=other):
            tile = pl.ds(128 * t, 128)
            c1[x, :, tile] = c1[x, :, tile] + v * other[x, :, tile]

        second_z(field, zmat, add)


def image_kernel(
    u2, b2, ylo, yhi, inner, outer, l2, d2, a1, c1, near, far, opposite, beside, padu, padb, total, chunks,
):
    for f, (pad, w) in enumerate(((padu, u2), (padb, b2))):
        fill(pad, w, inner, outer, f)
    nx = u2.shape[0]
    for x in range(nx):
        hu, hb = (
            lateral(pad, x, edge_rows(ylo, yhi, x, f, nx // 2), False)[0] for f, pad in enumerate((padu, padb))
        )
        for t in (0, 1):
            tile = pl.ds(128 * t, 128)
            total[x, :, tile] = a1[x, :, tile] + hu[t] * d2[x, :, tile] + hb[t] * l2[x, :, tile]
    lane = lanes()
    group = nx // 4
    for i in range(group):
        for f, array in enumerate((total, c1)):
            for t in (0, 1):
                parts = [array[g * group + i, :, pl.ds(128 * t, 128)] for g in range(4)]
                for k in range(4):
                    a, b, c, d = (
                        pltpu.roll(part, (32 * (g - k)) % 128, 1) if g != k else part
                        for g, part in enumerate(parts)
                    )
                    chunks[4 * t + k, f * group + i] = jnp.where(
                        lane < 32, a, jnp.where(lane < 64, b, jnp.where(lane < 96, c, d))
                    )
    shot = lax.axis_index("shot")
    y, xh = shot // 2, lax.rem(shot, 2)

    def chunk_at(step, same):
        return chunks[lax.rem(y + step, 4) * 2 + (xh if same else 1 - xh)]

    for out, wanted in (
        (near, ((0, True), (0, False))),
        (far, ((1, True), (3, True))),
        (opposite, ((2, True), (2, False))),
        (beside, ((1, False), (3, False))),
    ):
        for i, (step, same) in enumerate(wanted):
            out[i] = chunk_at(step, same)


def add_kernel(here, arrived, *outs):
    for i, out in enumerate(outs):
        out[...] = here[i] + arrived[i]


def sum_kernel(speed, epsilon, delta, own, other, up, down, out):
    group = out.shape[1] // 4
    tile, shift = own_depth(lax.axis_index("shot"))
    for i in range(group):
        sums = []
        for f in (0, 1):
            j = f * group + i
            sums.append((own[j] + other[j]) + (up[j] + down[j]))
        for g in range(4):
            x = g * group + i
            a, c = (pltpu.roll(v, (128 - 32 * g) % 128, 1) if g else v for v in sums)
            s, e, d = (pltpu.roll(w[x, :, tile], shift, 1) for w in (speed, epsilon, delta))
            out[0, x] = (e * a + d * c)[:, 0:32]
            out[1, x] = (s * a)[:, 0:32]
            out[2, x] = (s * c)[:, 0:32]


def per_device(
    speed, epsilon, delta, tilt, perturbation, forward_prev, forward_now, adjoint_prev, adjoint_now,
    wavelet, source_cell, receiver_cells,
):
    nx, ny, nz = speed.shape
    whole = (nx, ny, nz)
    pad = pltpu.VMEM((nx + 4, ny, nz), F32)
    half_rows = (nx // 2, ny, nz)
    layers = [half_rows] * 2 + [(4, ny, nz)] * 2
    packed = (nx // 2, ny, 128)
    model = (speed, epsilon, delta, tilt)

    def exchange_y(up, down):
        return cycle(up, "gy", 1), cycle(down, "gy", -1)

    def exchange_x(inner, outer):
        n = lax.axis_size("gx")
        return (
            lax.ppermute(inner, "gx", [(i, i ^ 1) for i in range(n)]),
            lax.ppermute(outer, "gx", [(i, ((i + 1) ^ 1) - 1 if 0 < i < n - 1 else n - 1 - i) for i in range(n)]),
        )

    now = (forward_now[0], adjoint_now[0])
    sent = pl.pallas_call(
        first_x_kernel,
        out_shape=[jax.ShapeDtypeStruct((4, ny, nz), F32)] * 2,
        in_specs=[pl.BlockSpec((8, ny, nz), lambda i, at=at: (at, 0, 0)) for at in (0, 0, nx // 8 - 1, nx // 8 - 1)],
        out_specs=[pl.BlockSpec((4, ny, nz), lambda i: (0, 0, 0))] * 2,
        grid=(1,),
        compiler_params=pltpu.CompilerParams(vmem_limit_bytes=LIMIT),
        name="layers_x",
    )(*now, *now)
    x0 = exchange_x(*sent)
    (mine,) = call(
        chunk_kernel,
        [packed],
        (perturbation, speed, epsilon, delta),
        [pltpu.VMEM((3, nx, ny, 128), F32)],
        after=sent,
        name="chunk",
    )
    partner, before, behind = across(mine), along(mine, 1), along(mine, -1)
    *sent, zmat = call(
        first_y_kernel, layers[:2] + [((2, nz, nz), BF16)], now, after=(mine, *x0), name="layers_y"
    )
    y0 = exchange_y(*sent)
    pair = jnp.concatenate([mine, partner], axis=0)
    opposite = along(pair, 2)
    beside = across(jnp.concatenate([before, behind], axis=0))
    (counts,) = call(
        functools.partial(counts_kernel, size_y=ny * lax.axis_size("gy"), depth=nz),
        [whole],
        (receiver_cells,),
        after=(pair, *sent),
        name="counts",
    )
    u1, l1, hu0, vu0, hl0, vl0 = call(
        first_kernel,
        [whole] * 6,
        (wavelet, source_cell, zmat, forward_now, forward_prev, adjoint_now, adjoint_prev) + y0 + x0 + model,
        [pad, pad],
        (0, 1),
        after=(counts,),
        name="first",
    )
    q1, q2, b1, d1, yup, ydn, inner_out, outer_out = call(
        born_kernel,
        [whole] * 4 + layers[:2] + [(8, ny, nz)] * 2,
        (mine, partner, before, behind, opposite, beside, u1, l1, hu0, vu0, hl0, vl0),
        [pltpu.VMEM((8, nx // 2, ny, 128), F32)],
        name="born",
    )
    y_ub = exchange_y(yup, ydn)
    x1 = exchange_x(inner_out, outer_out)
    y_ld = exchange_y(*call(y_kernel, layers[:2], (l1, d1), name="adjoint_y"))
    u2, b2, hu1, vu1, hb1, vb1, yup, ydn, inner_out, outer_out = call(
        second_kernel,
        [whole] * 6 + layers,
        (wavelet, source_cell, zmat, forward_now, u1, b1, q1, q2) + y_ub + x1 + model,
        [pad, pad],
        (0, 1),
        name="second",
    )
    halo = exchange_y(yup, ydn) + exchange_x(inner_out, outer_out)
    l2, d2, a1, c1 = call(
        adjoint_kernel,
        [whole] * 4,
        (zmat, adjoint_now, l1, d1, b1, q1, q2, counts, hu1, vu1, hb1, vb1, u2, b2) + y_ld + x1 + model,
        [pad, pad, pltpu.VMEM(whole, F32), pltpu.VMEM(whole, F32)],
        name="adjoint",
    )
    near, far, opposite, beside = call(
        image_kernel,
        [(2,) + packed] * 4,
        (u2, b2) + halo + (l2, d2, a1, c1),
        [pad, pad, pltpu.VMEM(whole, F32), pltpu.VMEM((8,) + packed, F32)],
        name="image",
    )
    own, other = call(add_kernel, [packed] * 2, (near, along(opposite, 2)), name="add_opposite")
    up, down = call(add_kernel, [packed] * 2, (far, across(beside)), name="add_beside")
    (out,) = call(
        sum_kernel,
        [(3, nx, ny, nz // 8)],
        model[:3] + (own, across(other), along(up, 1), along(down, -1)),
        name="sum",
    )
    return out


def solution(mesh):
    placed = (
        P("gx", "gy", None),
        P("gx", "gy", None),
        P("gx", "gy", None),
        P("gx", "gy", None),
        P(None, "gx", "gy", "shot"),
        P("shot", "gx", "gy", None),
        P("shot", "gx", "gy", None),
        P("shot", "gx", "gy", None),
        P("shot", "gx", "gy", None),
        P("shot", None),
        P("shot"),
        P("shot", None),
    )
    return jax.shard_map(
        per_device,
        mesh=mesh,
        in_specs=placed,
        out_specs=P(None, "gx", "gy", "shot"),
        check_vma=False,
    )
```

```python
import functools

import jax
import jax.numpy as jnp
from jax import lax
from jax.experimental import pallas as pl
from jax.experimental.pallas import tpu as pltpu
from jax.sharding import PartitionSpec as P

F32 = jnp.float32
BF16 = jnp.bfloat16
GROUP = 16
LIMIT = 24 * 1024 * 1024

S0, S1, S2 = -2.5, 4.0 / 3.0, -1.0 / 12.0
D1, D2 = 2.0 / 3.0, -1.0 / 12.0


def call(kernel, outs, ins, scratch=(), after=(), name=None):
    places = [pltpu.VMEM] * len(ins) + [pl.ANY] * len(after)
    typed = [out if out[-1] is BF16 else (out, F32) for out in outs]
    return pl.pallas_call(
        kernel,
        out_shape=[jax.ShapeDtypeStruct(*out) for out in typed],
        in_specs=[pl.BlockSpec(memory_space=place) for place in places],
        out_specs=[pl.BlockSpec(memory_space=pltpu.VMEM)] * len(outs),
        scratch_shapes=list(scratch),
        compiler_params=pltpu.CompilerParams(vmem_limit_bytes=LIMIT),
        name=name,
    )(*ins, *after)


def pairs(value, axis, outer=False):
    n = lax.axis_size(axis)
    other = [i ^ 1 if not outer else (((i + 1) % n ^ 1) - 1) % n for i in range(n)]
    return lax.ppermute(value, axis, list(enumerate(other)))


def outer_y(value):
    nx, ny = lax.axis_size("gx"), lax.axis_size("gy")
    swaps = []
    for x in range(nx):
        for y in range(ny):
            there = (x ^ 1, y) if y in (0, ny - 1) else (x, ((y + 1) ^ 1) - 1)
            swaps.append((x * ny + y, there[0] * ny + there[1]))
    return lax.ppermute(value, ("gx", "gy"), swaps)


def across(value):
    return lax.ppermute(value, "shot", [(i, i ^ 1) for i in range(8)])


def opposite_y(value):
    return lax.ppermute(value, "shot", [(i, (i + 4) % 8) for i in range(8)])


def beside_y(value, outer=False):
    return lax.ppermute(value, "shot", [(i, neighbour(i // 2, outer) * 2 + i % 2) for i in range(8)])


def neighbour(y, outer):
    return (y ^ 1) if not outer else (((y + 1) & 3) ^ 1) + 3 & 3


def rows():
    return lax.broadcasted_iota(jnp.int32, (8, 128), 0)


def lanes():
    return lax.broadcasted_iota(jnp.int32, (8, 128), 1)


def even(axis):
    return lax.rem(lax.axis_index(axis), 2) == 0


def pack_y(fields, inner, outer):
    row = rows()
    nx = fields[0].shape[0]
    base = jnp.where(even("gy"), 6, 0)
    for out, base in ((inner, base), (outer, 6 - base)):
        for i in range(nx // 2):
            for h in (0, 128):
                tile = pl.ds(h, 128)
                acc = None
                for piece in (0, 1):
                    for f, field in enumerate(fields):
                        at = 4 * piece + 2 * f
                        value = pltpu.roll(field[i + piece * (nx // 2), :, tile], lax.rem(at + 8 - base, 8), 0)
                        acc = value if acc is None else jnp.where(row >= at, value, acc)
                out[i, :, tile] = acc


def face_x(first, last, inner, outer, f):
    at_even = even("gx")
    inner[2 * f : 2 * f + 2] = jnp.where(at_even, last, first)
    outer[2 * f : 2 * f + 2] = jnp.where(at_even, first, last)


def pack_x(fields, inner, outer):
    for f, field in enumerate(fields):
        n = field.shape[0]
        face_x(field[0:2], field[n - 2 : n], inner, outer, f)


def fill(pad, field, inner, outer, f):
    n = field.shape[0]
    gx, at_even = lax.axis_index("gx"), even("gx")
    inner, outer = inner[2 * f : 2 * f + 2], outer[2 * f : 2 * f + 2]
    pad[2 : n + 2] = field[...]
    pad[0:2] = jnp.where(gx > 0, jnp.where(at_even, outer, inner), 0.0)
    pad[n + 2 : n + 4] = jnp.where(gx < lax.axis_size("gx") - 1, jnp.where(at_even, inner, outer), 0.0)


def edge_rows(inner, outer, x, f, half):
    row = rows()
    gy, n = lax.axis_index("gy"), lax.axis_size("gy")
    low = jnp.where(even("gy"), 0, 6)
    from_inner = (row >= low) & (row < low + 2)
    from_outer = (row >= 6 - low) & (row < 8 - low) & (gy > 0) & (gy < n - 1)
    i, at = x % half, 4 * (x // half) + 2 * f
    out = []
    for t in (0, 1):
        tile = pl.ds(128 * t, 128)
        near = pltpu.roll(inner[i, :, tile], lax.rem(low + 8 - at, 8), 0)
        far = pltpu.roll(outer[i, :, tile], lax.rem(14 - low - at, 8), 0)
        out.append(jnp.where(from_inner, near, jnp.where(from_outer, far, 0.0)))
    return out


def along_z(values, matrix):
    total = None
    for _ in range(3):
        part = values.astype(BF16)
        values = values - part.astype(F32)
        term = jnp.dot(part, matrix, preferred_element_type=F32)
        total = term if total is None else total + term
    return total * (1.0 / 12.0)


def lateral(pad, x, edge, slope=True):
    row = rows()
    horizontal, slopes, centre = [], [], []
    for t in (0, 1):
        tile = pl.ds(128 * t, 128)
        c = pad[x + 2, :, tile]
        xl, xh, xl2, xh2 = (pad[x + k, :, tile] for k in (1, 3, 0, 4))
        e = edge[t]
        yl = pltpu.roll(jnp.where(row == 7, e, c), 1, 0)
        yl2 = pltpu.roll(jnp.where(row >= 6, e, c), 2, 0)
        yh = pltpu.roll(jnp.where(row == 0, e, c), 7, 0)
        yh2 = pltpu.roll(jnp.where(row <= 1, e, c), 6, 0)
        horizontal.append(2.0 * S0 * c + S1 * ((xl + xh) + (yl + yh)) + S2 * ((xl2 + xh2) + (yl2 + yh2)))
        if slope:
            slopes.append(D1 * ((xh - xl) + (yh - yl)) + D2 * ((xh2 - xl2) + (yh2 - yl2)))
        centre.append(c)
    return horizontal, slopes, centre


def slabs(lists):
    return jnp.concatenate([jnp.concatenate(pair, axis=1) for pair in lists], axis=0)


def derivs(pad, before, after, f, zmat, emit):
    nx = pad.shape[0] - 4
    for at in range(0, nx, GROUP):
        found = [lateral(pad, x, edge_rows(before, after, x, f, nx // 2)) for x in range(at, at + GROUP)]
        vertical = along_z(slabs([c for _, _, c in found]), zmat[0])
        mixed = along_z(slabs([s for _, s, _ in found]), zmat[1])
        for j, (horizontal, _, centre) in enumerate(found):
            for t in (0, 1):
                part = (slice(8 * j, 8 * j + 8), slice(128 * t, 128 * t + 128))
                emit(at + j, t, horizontal[t], vertical[part], mixed[part], centre[t])


def second_z(field, zmat, emit):
    for at in range(0, field.shape[0], GROUP):
        vertical = along_z(field[at : at + GROUP].reshape(GROUP * 8, field.shape[2]), zmat[0])
        for j in range(GROUP):
            for t in (0, 1):
                emit(at + j, t, vertical[8 * j : 8 * j + 8, 128 * t : 128 * t + 128])


def operate(model, x, tile, h, v, m):
    s, e, d, k = (w[x, :, tile] for w in model)
    return s * (e * h + d * v) + k * m


def z_matrices(out):
    shape = out.shape[1:]
    offset = lax.broadcasted_iota(jnp.int32, shape, 0) - lax.broadcasted_iota(jnp.int32, shape, 1)
    far = jnp.abs(offset)
    second = jnp.where(far == 0, -30.0, jnp.where(far == 1, 16.0, jnp.where(far == 2, -1.0, 0.0)))
    first = jnp.where(far == 1, 8.0, jnp.where(far == 2, -1.0, 0.0))
    out[0] = second.astype(BF16)
    out[1] = jnp.where(offset > 0, first, -first).astype(BF16)


def own_depth(shot):
    tile = pl.ds(pl.multiple_of((shot // 4) * 128, 128), 128)
    return tile, lax.rem(128 - 32 * lax.rem(shot, 4), 128)


def chunk_kernel(p, speed, other, *rest, which):
    before, (chunk, first, second) = rest[:-3], rest[-3:]
    first[:, :, 0:32] = p[0]
    second[:, :, 0:32] = p[which]
    tile, shift = own_depth(lax.axis_index("shot"))
    lane = lanes()
    group = first.shape[0] // 4
    start = 0
    if before:
        start = group
        chunk[0:group] = before[0][...]
    for i in range(group):
        parts = []
        for g in range(4):
            x = g * group + i
            s, e = (pltpu.roll(w[x, :, tile], shift, 1) for w in (speed, other))
            q = first[x] * e + s * second[x]
            parts.append(pltpu.roll(q, 32 * g, 1) if g else q)
        a, b, c, d = parts
        chunk[start + i] = jnp.where(lane < 32, a, jnp.where(lane < 64, b, jnp.where(lane < 96, c, d)))


def first_x_kernel(u_first, l_first, u_last, l_last, inner, outer):
    for f, (first, last) in enumerate(((u_first, u_last), (l_first, l_last))):
        face_x(first[0:2], last[6:8], inner, outer, f)


def first_y_kernel(u, l, *rest):
    up, down, zmat = rest[-3:]
    pack_y([u, l], up, down)
    z_matrices(zmat)


def y_kernel(a, b, up, down):
    pack_y([a, b], up, down)


def first_kernel(
    plane, zmat, u, um, l, lm, ylo, yhi, inner, outer, speed, epsilon, delta, tilt,
    u1, l1, hu, vu, hl, vl, padu, padl,
):
    model = (speed, epsilon, delta, tilt)
    for f, (pad, w, prev, new, h_out, v_out) in enumerate(
        ((padu, u, um, u1, hu, vu), (padl, l, lm, l1, hl, vl))
    ):
        fill(pad, w.at[0], inner, outer, f)

        def emit(x, t, h, v, m, c, f=f, prev=prev, new=new, h_out=h_out, v_out=v_out):
            tile = pl.ds(128 * t, 128)
            h_out[x, :, tile] = h
            v_out[x, :, tile] = v
            value = 2.0 * c - prev[0, x, :, tile] + operate(model, x, tile, h, v, m)
            if f == 0:
                value = value + plane[0, :, tile]
            new[x, :, tile] = value

        derivs(pad, ylo, yhi, f, zmat, emit)


def born_kernel(
    mine, partner, inner, outer, opposite, beside, u1, l1, hu, vu, hl, vl, q1, q2, b1, d1, yup, ydn, inner_out, outer_out, chunks,
):
    shot = lax.axis_index("shot")
    y, xh = shot // 2, lax.rem(shot, 2)
    group = hu.shape[0] // 4
    n = 2 * group
    for there, same, other in (
        (y, mine[...], partner[...]),
        (neighbour(y, False), inner[...], beside[0:n]),
        (neighbour(y, True), outer[...], beside[n : 2 * n]),
        (y ^ 2, opposite[0:n], opposite[n : 2 * n]),
    ):
        chunks[there * 2 + xh] = same
        chunks[there * 2 + 1 - xh] = other
    lane = lanes()
    for x in range(4 * group):
        g, i = x // group, x % group
        for t in (0, 1):
            tile = pl.ds(128 * t, 128)
            both = []
            for f in (0, 1):
                parts = []
                for k in range(4):
                    part = chunks[4 * t + k, f * group + i]
                    parts.append(pltpu.roll(part, (32 * (k - g)) % 128, 1) if k != g else part)
                a, b, c, d = parts
                both.append(jnp.where(lane < 32, a, jnp.where(lane < 64, b, jnp.where(lane < 96, c, d))))
            q1[x, :, tile], q2[x, :, tile] = both
            b1[x, :, tile] = both[0] * hu[x, :, tile] + both[1] * vu[x, :, tile]
            d1[x, :, tile] = both[0] * hl[x, :, tile] + both[1] * vl[x, :, tile]
    pack_y([u1, b1], yup, ydn)
    pack_x([u1, b1, l1, d1], inner_out, outer_out)


def second_kernel(
    plane, zmat, u, u1, b1, q1, q2, ylo, yhi, inner, outer, speed, epsilon, delta, tilt,
    u2, b2, hu, vu, hb, vb, yup, ydn, inner_out, outer_out, padu, padb,
):
    model = (speed, epsilon, delta, tilt)
    fill(padu, u1, inner, outer, 0)
    fill(padb, b1, inner, outer, 1)

    def emit_u(x, t, h, v, m, c):
        tile = pl.ds(128 * t, 128)
        hu[x, :, tile] = h
        vu[x, :, tile] = v
        u2[x, :, tile] = (
            2.0 * c - u[0, x, :, tile] + operate(model, x, tile, h, v, m)
            + plane[1, :, tile]
        )

    def emit_b(x, t, h, v, m, c):
        tile = pl.ds(128 * t, 128)
        hb[x, :, tile] = h
        vb[x, :, tile] = v
        b2[x, :, tile] = (
            2.0 * c + operate(model, x, tile, h, v, m)
            + (q1[x, :, tile] * hu[x, :, tile] + q2[x, :, tile] * vu[x, :, tile])
        )

    derivs(padu, ylo, yhi, 0, zmat, emit_u)
    derivs(padb, ylo, yhi, 1, zmat, emit_b)
    fields = [u2, b2]
    pack_y(fields, yup, ydn)
    pack_x(fields, inner_out, outer_out)


def counts_kernel(cells, wavelet, source, *rest, size_y, depth):
    out, plane, amounts, place, sems = rest[-5:]
    copies = [
        pltpu.make_async_copy(wavelet, amounts, sems.at[0]),
        pltpu.make_async_copy(source, place, sems.at[1]),
    ]
    for copy in copies:
        copy.start()
    nx, ny = out.shape[0], out.shape[1]
    gx, gy = lax.axis_index("gx"), lax.axis_index("gy")
    index = cells[...]
    cx = lax.div(index, size_y * depth) - gx * nx
    cy = lax.rem(lax.div(index, depth), size_y) - gy * ny
    cz = lax.rem(index, depth)
    inside = (cx >= 0) & (cx < nx) & (cy >= 0) & (cy < ny)
    at = jnp.where(inside, cx * ny + cy, -1)
    n = index.shape[1]
    left = jnp.where(lax.broadcasted_iota(jnp.int32, (nx * ny, n), 0) == at, 1.0, 0.0).astype(BF16)
    right = jnp.where(lax.broadcasted_iota(jnp.int32, (depth, n), 0) == cz, 1.0, 0.0).astype(BF16)
    total = lax.dot_general(left, right, (((1,), (1,)), ((), ())), preferred_element_type=F32)
    out[...] = total.reshape(nx, ny, depth)
    for copy in copies:
        copy.wait()
    cell = lax.broadcasted_iota(jnp.int32, (ny, depth), 1)
    for step in range(plane.shape[0]):
        plane[step] = jnp.where(cell == place[0], amounts[0, step], 0.0)


def adjoint_kernel(
    zmat, l, l1, d1, b1, q1, q2, counts, hu, vu, hb, vb, u2, b2, ylo, yhi, inner, outer,
    speed, epsilon, delta, tilt, l2, d2, a1, c1, padl, padd, hl, vl,
):
    model = (speed, epsilon, delta, tilt)
    fill(padl, l1, inner, outer, 2)
    fill(padd, d1, inner, outer, 3)

    def emit_l(x, t, h, v, m, c):
        tile = pl.ds(128 * t, 128)
        hl[x, :, tile] = h
        vl[x, :, tile] = v
        l2[x, :, tile] = 2.0 * c - l[0, x, :, tile] + operate(model, x, tile, h, v, m)

    def emit_d(x, t, h, v, m, c):
        tile = pl.ds(128 * t, 128)
        d2[x, :, tile] = (
            2.0 * c + operate(model, x, tile, h, v, m)
            + (q1[x, :, tile] * hl[x, :, tile] + q2[x, :, tile] * vl[x, :, tile])
            + counts[x, :, tile] * b1[x, :, tile]
        )
        a1[x, :, tile] = hu[x, :, tile] * c + hb[x, :, tile] * l1[x, :, tile]
        c1[x, :, tile] = vu[x, :, tile] * c + vb[x, :, tile] * l1[x, :, tile]

    derivs(padl, ylo, yhi, 0, zmat, emit_l)
    derivs(padd, ylo, yhi, 1, zmat, emit_d)

    for field, other in ((u2, d2), (b2, l2)):

        def add(x, t, v, other=other):
            tile = pl.ds(128 * t, 128)
            c1[x, :, tile] = c1[x, :, tile] + v * other[x, :, tile]

        second_z(field, zmat, add)


def image_kernel(
    u2, b2, ylo, yhi, inner, outer, l2, d2, a1, c1, near, far, opposite, beside, padu, padb, total, chunks,
):
    for f, (pad, w) in enumerate(((padu, u2), (padb, b2))):
        fill(pad, w, inner, outer, f)
    nx = u2.shape[0]
    for x in range(nx):
        hu, hb = (
            lateral(pad, x, edge_rows(ylo, yhi, x, f, nx // 2), False)[0] for f, pad in enumerate((padu, padb))
        )
        for t in (0, 1):
            tile = pl.ds(128 * t, 128)
            total[x, :, tile] = a1[x, :, tile] + hu[t] * d2[x, :, tile] + hb[t] * l2[x, :, tile]
    lane = lanes()
    group = nx // 4
    for i in range(group):
        for f, array in enumerate((total, c1)):
            for t in (0, 1):
                parts = [array[g * group + i, :, pl.ds(128 * t, 128)] for g in range(4)]
                for k in range(4):
                    a, b, c, d = (
                        pltpu.roll(part, (32 * (g - k)) % 128, 1) if g != k else part
                        for g, part in enumerate(parts)
                    )
                    chunks[4 * t + k, f * group + i] = jnp.where(
                        lane < 32, a, jnp.where(lane < 64, b, jnp.where(lane < 96, c, d))
                    )
    shot = lax.axis_index("shot")
    y, xh = shot // 2, lax.rem(shot, 2)

    def chunk_at(there, same):
        return chunks[there * 2 + (xh if same else 1 - xh)]

    inner_y, outer_y = neighbour(y, False), neighbour(y, True)

    for out, wanted in (
        (near, ((y, True), (y, False))),
        (far, ((inner_y, True), (outer_y, True))),
        (opposite, ((y ^ 2, True), (y ^ 2, False))),
        (beside, ((inner_y, False), (outer_y, False))),
    ):
        for i, (there, same) in enumerate(wanted):
            out[i] = chunk_at(there, same)


def add_kernel(here, arrived, *outs):
    for i, out in enumerate(outs):
        out[...] = here[i] + arrived[i]


def sum_kernel(speed, epsilon, delta, own, other, up, down, out):
    group = out.shape[1] // 4
    tile, shift = own_depth(lax.axis_index("shot"))
    for i in range(group):
        sums = []
        for f in (0, 1):
            j = f * group + i
            sums.append((own[j] + other[j]) + (up[j] + down[j]))
        for g in range(4):
            x = g * group + i
            a, c = (pltpu.roll(v, (128 - 32 * g) % 128, 1) if g else v for v in sums)
            s, e, d = (pltpu.roll(w[x, :, tile], shift, 1) for w in (speed, epsilon, delta))
            out[0, x] = (e * a + d * c)[:, 0:32]
            out[1, x] = (s * a)[:, 0:32]
            out[2, x] = (s * c)[:, 0:32]


def per_device(
    speed, epsilon, delta, tilt, perturbation, forward_prev, forward_now, adjoint_prev, adjoint_now,
    wavelet, source_cell, receiver_cells,
):
    nx, ny, nz = speed.shape
    whole = (nx, ny, nz)
    pad = pltpu.VMEM((nx + 4, ny, nz), F32)
    half_rows = (nx // 2, ny, nz)
    layers = [half_rows] * 2 + [(4, ny, nz)] * 2
    packed = (nx // 2, ny, 128)
    model = (speed, epsilon, delta, tilt)

    def exchange_y(inner, outer):
        outer = outer_y(outer)
        return pairs(inner, "gy"), outer

    def exchange_x(inner, outer):
        outer = pairs(outer, "gx", True)
        return pairs(inner, "gx"), outer

    now = (forward_now[0], adjoint_now[0])
    (half,) = call(
        functools.partial(chunk_kernel, which=1),
        [(nx // 4, ny, 128)],
        (perturbation, speed, epsilon),
        [pltpu.VMEM((nx, ny, 128), F32)] * 2,
        name="half_chunk",
    )
    sent = pl.pallas_call(
        first_x_kernel,
        out_shape=[jax.ShapeDtypeStruct((4, ny, nz), F32)] * 2,
        in_specs=[pl.BlockSpec((8, ny, nz), lambda i, at=at: (at, 0, 0)) for at in (0, 0, nx // 8 - 1, nx // 8 - 1)],
        out_specs=[pl.BlockSpec((4, ny, nz), lambda i: (0, 0, 0))] * 2,
        grid=(1,),
        compiler_params=pltpu.CompilerParams(vmem_limit_bytes=LIMIT),
        name="layers_x",
    )(*now, *now)
    x0 = exchange_x(*sent)
    (mine,) = call(
        functools.partial(chunk_kernel, which=2),
        [packed],
        (perturbation, speed, delta, half),
        [pltpu.VMEM((nx, ny, 128), F32)] * 2,
        name="chunk",
    )
    partner, inner, outer = across(mine), beside_y(mine), beside_y(mine, True)
    *sent, zmat = call(
        first_y_kernel, layers[:2] + [((2, nz, nz), BF16)], now, after=(mine, *x0), name="layers_y"
    )
    y0 = exchange_y(*sent)
    pair = jnp.concatenate([mine, partner], axis=0)
    opposite = opposite_y(pair)
    beside = across(jnp.concatenate([inner, outer], axis=0))
    steps = wavelet.shape[1]
    counts, plane = call(
        functools.partial(counts_kernel, size_y=ny * lax.axis_size("gy"), depth=nz),
        [whole, (steps, ny, nz)],
        (receiver_cells,),
        [pltpu.SMEM((1, steps), F32), pltpu.SMEM((1,), jnp.int32), pltpu.SemaphoreType.DMA((2,))],
        after=(wavelet, source_cell, pair, *sent),
        name="counts",
    )
    u1, l1, hu0, vu0, hl0, vl0 = call(
        first_kernel,
        [whole] * 6,
        (plane, zmat, forward_now, forward_prev, adjoint_now, adjoint_prev) + y0 + x0 + model,
        [pad, pad],
        name="first",
    )
    q1, q2, b1, d1, yup, ydn, inner_out, outer_out = call(
        born_kernel,
        [whole] * 4 + layers[:2] + [(8, ny, nz)] * 2,
        (mine, partner, inner, outer, opposite, beside, u1, l1, hu0, vu0, hl0, vl0),
        [pltpu.VMEM((8, nx // 2, ny, 128), F32)],
        name="born",
    )
    y_ub = exchange_y(yup, ydn)
    x1 = exchange_x(inner_out, outer_out)
    y_ld = exchange_y(*call(y_kernel, layers[:2], (l1, d1), name="adjoint_y"))
    u2, b2, hu1, vu1, hb1, vb1, yup, ydn, inner_out, outer_out = call(
        second_kernel,
        [whole] * 6 + layers,
        (plane, zmat, forward_now, u1, b1, q1, q2) + y_ub + x1 + model,
        [pad, pad],
        name="second",
    )
    halo = exchange_y(yup, ydn) + exchange_x(inner_out, outer_out)
    l2, d2, a1, c1 = call(
        adjoint_kernel,
        [whole] * 4,
        (zmat, adjoint_now, l1, d1, b1, q1, q2, counts, hu1, vu1, hb1, vb1, u2, b2) + y_ld + x1 + model,
        [pad, pad, pltpu.VMEM(whole, F32), pltpu.VMEM(whole, F32)],
        name="adjoint",
    )
    near, far, opposite, beside = call(
        image_kernel,
        [(2,) + packed] * 4,
        (u2, b2) + halo + (l2, d2, a1, c1),
        [pad, pad, pltpu.VMEM(whole, F32), pltpu.VMEM((8,) + packed, F32)],
        name="image",
    )
    own, other = call(add_kernel, [packed] * 2, (near, opposite_y(opposite)), name="add_opposite")
    inner, outer = call(add_kernel, [packed] * 2, (far, across(beside)), name="add_beside")
    (out,) = call(
        sum_kernel,
        [(3, nx, ny, nz // 8)],
        model[:3] + (own, across(other), beside_y(inner), beside_y(outer, True)),
        name="sum",
    )
    return out


def solution(mesh):
    placed = (
        P("gx", "gy", None),
        P("gx", "gy", None),
        P("gx", "gy", None),
        P("gx", "gy", None),
        P(None, "gx", "gy", "shot"),
        P("shot", "gx", "gy", None),
        P("shot", "gx", "gy", None),
        P("shot", "gx", "gy", None),
        P("shot", "gx", "gy", None),
        P("shot", None),
        P("shot"),
        P("shot", None),
    )
    return jax.shard_map(
        per_device,
        mesh=mesh,
        in_specs=placed,
        out_specs=P(None, "gx", "gy", "shot"),
        check_vma=False,
    )
```

```python
import functools

import jax
import jax.numpy as jnp
from jax import lax
from jax.experimental import pallas as pl
from jax.experimental.pallas import tpu as pltpu
from jax.sharding import PartitionSpec as P

F32 = jnp.float32
BF16 = jnp.bfloat16
GROUP = 24
LIMIT = 24 * 1024 * 1024

S0, S1, S2 = -2.5, 4.0 / 3.0, -1.0 / 12.0
D1, D2 = 2.0 / 3.0, -1.0 / 12.0


def call(kernel, outs, ins, scratch=(), after=(), name=None):
    places = [pltpu.VMEM] * len(ins) + [pl.ANY] * len(after)
    typed = [out if out[-1] is BF16 else (out, F32) for out in outs]
    return pl.pallas_call(
        kernel,
        out_shape=[jax.ShapeDtypeStruct(*out) for out in typed],
        in_specs=[pl.BlockSpec(memory_space=place) for place in places],
        out_specs=[pl.BlockSpec(memory_space=pltpu.VMEM)] * len(outs),
        scratch_shapes=list(scratch),
        compiler_params=pltpu.CompilerParams(vmem_limit_bytes=LIMIT),
        name=name,
    )(*ins, *after)


def pairs(value, axis, outer=False):
    n = lax.axis_size(axis)
    other = [i ^ 1 if not outer else (((i + 1) % n ^ 1) - 1) % n for i in range(n)]
    return lax.ppermute(value, axis, list(enumerate(other)))


def outer_y(value):
    nx, ny = lax.axis_size("gx"), lax.axis_size("gy")
    swaps = []
    for x in range(nx):
        for y in range(ny):
            there = (x ^ 1, y) if y in (0, ny - 1) else (x, ((y + 1) ^ 1) - 1)
            swaps.append((x * ny + y, there[0] * ny + there[1]))
    return lax.ppermute(value, ("gx", "gy"), swaps)


def across(value):
    return lax.ppermute(value, "shot", [(i, i ^ 1) for i in range(8)])


def opposite_y(value):
    return lax.ppermute(value, "shot", [(i, (i + 4) % 8) for i in range(8)])


def beside_y(value, outer=False):
    return lax.ppermute(value, "shot", [(i, neighbour(i // 2, outer) * 2 + i % 2) for i in range(8)])


def neighbour(y, outer):
    return (y ^ 1) if not outer else (((y + 1) & 3) ^ 1) + 3 & 3


def rows():
    return lax.broadcasted_iota(jnp.int32, (8, 128), 0)


def lanes():
    return lax.broadcasted_iota(jnp.int32, (8, 128), 1)


def even(axis):
    return lax.rem(lax.axis_index(axis), 2) == 0


def pack_y(fields, inner, outer):
    row = rows()
    nx = fields[0].shape[0]
    base = jnp.where(even("gy"), 6, 0)
    for out, base in ((inner, base), (outer, 6 - base)):
        for i in range(nx // 2):
            for h in (0, 128):
                tile = pl.ds(h, 128)
                acc = None
                for piece in (0, 1):
                    for f, field in enumerate(fields):
                        at = 4 * piece + 2 * f
                        value = pltpu.roll(field[i + piece * (nx // 2), :, tile], lax.rem(at + 8 - base, 8), 0)
                        acc = value if acc is None else jnp.where(row >= at, value, acc)
                out[i, :, tile] = acc


def face_x(first, last, inner, outer, f):
    at_even = even("gx")
    inner[2 * f : 2 * f + 2] = jnp.where(at_even, last, first)
    outer[2 * f : 2 * f + 2] = jnp.where(at_even, first, last)


def pack_x(fields, inner, outer):
    for f, field in enumerate(fields):
        n = field.shape[0]
        face_x(field[0:2], field[n - 2 : n], inner, outer, f)


def extended(field, inner, outer, f):
    n = field.shape[0]
    gx, at_even = lax.axis_index("gx"), even("gx")
    inner, outer = inner[2 * f : 2 * f + 2], outer[2 * f : 2 * f + 2]
    before = jnp.where(gx > 0, jnp.where(at_even, outer, inner), 0.0)
    after = jnp.where(gx < lax.axis_size("gx") - 1, jnp.where(at_even, inner, outer), 0.0)

    def slab(x, t):
        if 0 <= x < n:
            return field[x, :, pl.ds(128 * t, 128)]
        return (before[x + 2] if x < 0 else after[x - n])[:, 128 * t : 128 * t + 128]

    return slab


def edge_rows(inner, outer, x, f, half):
    row = rows()
    gy, n = lax.axis_index("gy"), lax.axis_size("gy")
    low = jnp.where(even("gy"), 0, 6)
    from_inner = (row >= low) & (row < low + 2)
    from_outer = (row >= 6 - low) & (row < 8 - low) & (gy > 0) & (gy < n - 1)
    i, at = x % half, 4 * (x // half) + 2 * f
    out = []
    for t in (0, 1):
        tile = pl.ds(128 * t, 128)
        near = pltpu.roll(inner[i, :, tile], lax.rem(low + 8 - at, 8), 0)
        far = pltpu.roll(outer[i, :, tile], lax.rem(14 - low - at, 8), 0)
        out.append(jnp.where(from_inner, near, jnp.where(from_outer, far, 0.0)))
    return out


def along_z(values, matrix):
    total = None
    for _ in range(3):
        part = values.astype(BF16)
        values = values - part.astype(F32)
        term = jnp.dot(part, matrix, preferred_element_type=F32)
        total = term if total is None else total + term
    return total


def lateral(slab, x, edge, slope=True):
    row = rows()
    horizontal, slopes, centre = [], [], []
    for t in (0, 1):
        c, xl, xh, xl2, xh2 = (slab(x + k, t) for k in (0, -1, 1, -2, 2))
        e = edge[t]
        yl = pltpu.roll(jnp.where(row == 7, e, c), 1, 0)
        yl2 = pltpu.roll(jnp.where(row >= 6, e, c), 2, 0)
        yh = pltpu.roll(jnp.where(row == 0, e, c), 7, 0)
        yh2 = pltpu.roll(jnp.where(row <= 1, e, c), 6, 0)
        horizontal.append(2.0 * S0 * c + S1 * ((xl + xh) + (yl + yh)) + S2 * ((xl2 + xh2) + (yl2 + yh2)))
        if slope:
            slopes.append((D1 / 12.0) * ((xh - xl) + (yh - yl)) + (D2 / 12.0) * ((xh2 - xl2) + (yh2 - yl2)))
        centre.append(c)
    return horizontal, slopes, centre


def slabs(lists):
    return jnp.concatenate([jnp.concatenate(pair, axis=1) for pair in lists], axis=0)


def derivs(slab, nx, before, after, f, zmat, emit):
    for at in range(0, nx, GROUP):
        found = [lateral(slab, x, edge_rows(before, after, x, f, nx // 2)) for x in range(at, at + GROUP)]
        vertical = along_z(slabs([c for _, _, c in found]), zmat[0]) * (1.0 / 12.0)
        mixed = along_z(slabs([s for _, s, _ in found]), zmat[1])
        for j, (horizontal, _, centre) in enumerate(found):
            for t in (0, 1):
                part = (slice(8 * j, 8 * j + 8), slice(128 * t, 128 * t + 128))
                emit(at + j, t, horizontal[t], vertical[part], mixed[part], centre[t])


def second_z(field, zmat, emit):
    for at in range(0, field.shape[0], GROUP):
        vertical = along_z(field[at : at + GROUP].reshape(GROUP * 8, field.shape[2]), zmat[0]) * (1.0 / 12.0)
        for j in range(GROUP):
            for t in (0, 1):
                emit(at + j, t, vertical[8 * j : 8 * j + 8, 128 * t : 128 * t + 128])


def operate(model, x, tile, h, v, m):
    s, e, d, k = (w[x, :, tile] for w in model)
    return s * (e * h + d * v) + k * m


def z_matrices(out):
    shape = out.shape[1:]
    offset = lax.broadcasted_iota(jnp.int32, shape, 0) - lax.broadcasted_iota(jnp.int32, shape, 1)
    far = jnp.abs(offset)
    second = jnp.where(far == 0, -30.0, jnp.where(far == 1, 16.0, jnp.where(far == 2, -1.0, 0.0)))
    first = jnp.where(far == 1, 8.0, jnp.where(far == 2, -1.0, 0.0))
    out[0] = second.astype(BF16)
    out[1] = jnp.where(offset > 0, first, -first).astype(BF16)


def own_depth(shot):
    tile = pl.ds(pl.multiple_of((shot // 4) * 128, 128), 128)
    return tile, lax.rem(128 - 32 * lax.rem(shot, 4), 128)


def chunk_kernel(p, speed, other, *rest, which):
    before, (chunk, first, second) = rest[:-3], rest[-3:]
    first[:, :, 0:32] = p[0]
    second[:, :, 0:32] = p[which]
    tile, shift = own_depth(lax.axis_index("shot"))
    lane = lanes()
    group = first.shape[0] // 4
    start = 0
    if before:
        start = group
        chunk[0:group] = before[0][...]
    for i in range(group):
        parts = []
        for g in range(4):
            x = g * group + i
            s, e = (pltpu.roll(w[x, :, tile], shift, 1) for w in (speed, other))
            q = first[x] * e + s * second[x]
            parts.append(pltpu.roll(q, 32 * g, 1) if g else q)
        a, b, c, d = parts
        chunk[start + i] = jnp.where(lane < 32, a, jnp.where(lane < 64, b, jnp.where(lane < 96, c, d)))


def first_x_kernel(u_first, l_first, u_last, l_last, inner, outer):
    for f, (first, last) in enumerate(((u_first, u_last), (l_first, l_last))):
        face_x(first[0:2], last[6:8], inner, outer, f)


def first_y_kernel(u, l, *rest):
    up, down, zmat = rest[-3:]
    pack_y([u, l], up, down)
    z_matrices(zmat)


def y_kernel(a, b, up, down):
    pack_y([a, b], up, down)


def first_kernel(
    plane, zmat, u, um, l, lm, ylo, yhi, inner, outer, speed, epsilon, delta, tilt,
    u1, l1, hu, vu, hl, vl,
):
    model = (speed, epsilon, delta, tilt)
    for f, (w, prev, new, h_out, v_out) in enumerate(((u, um, u1, hu, vu), (l, lm, l1, hl, vl))):

        def emit(x, t, h, v, m, c, f=f, prev=prev, new=new, h_out=h_out, v_out=v_out):
            tile = pl.ds(128 * t, 128)
            h_out[x, :, tile] = h
            v_out[x, :, tile] = v
            value = 2.0 * c - prev[0, x, :, tile] + operate(model, x, tile, h, v, m)
            if f == 0:
                value = value + plane[0, :, tile]
            new[x, :, tile] = value

        slab = extended(w.at[0], inner, outer, f)
        derivs(slab, w.shape[1], ylo, yhi, f, zmat, emit)


def born_kernel(
    mine, partner, inner, outer, opposite, beside, u1, l1, hu, vu, hl, vl, q1, q2, b1, d1, yup, ydn, inner_out, outer_out, chunks,
):
    shot = lax.axis_index("shot")
    y, xh = shot // 2, lax.rem(shot, 2)
    group = hu.shape[0] // 4
    n = 2 * group
    for there, same, other in (
        (y, mine[...], partner[...]),
        (neighbour(y, False), inner[...], beside[0:n]),
        (neighbour(y, True), outer[...], beside[n : 2 * n]),
        (y ^ 2, opposite[0:n], opposite[n : 2 * n]),
    ):
        chunks[there * 2 + xh] = same
        chunks[there * 2 + 1 - xh] = other
    lane = lanes()
    for x in range(4 * group):
        g, i = x // group, x % group
        for t in (0, 1):
            tile = pl.ds(128 * t, 128)
            both = []
            for f in (0, 1):
                parts = []
                for k in range(4):
                    part = chunks[4 * t + k, f * group + i]
                    parts.append(pltpu.roll(part, (32 * (k - g)) % 128, 1) if k != g else part)
                a, b, c, d = parts
                both.append(jnp.where(lane < 32, a, jnp.where(lane < 64, b, jnp.where(lane < 96, c, d))))
            q1[x, :, tile], q2[x, :, tile] = both
            b1[x, :, tile] = both[0] * hu[x, :, tile] + both[1] * vu[x, :, tile]
            d1[x, :, tile] = both[0] * hl[x, :, tile] + both[1] * vl[x, :, tile]
    pack_y([u1, b1], yup, ydn)
    pack_x([u1, b1, l1, d1], inner_out, outer_out)


def second_kernel(
    plane, zmat, u, u1, b1, q1, q2, ylo, yhi, inner, outer, speed, epsilon, delta, tilt,
    u2, b2, hu, vu, hb, vb, yup, ydn, inner_out, outer_out,
):
    model = (speed, epsilon, delta, tilt)

    def emit_u(x, t, h, v, m, c):
        tile = pl.ds(128 * t, 128)
        hu[x, :, tile] = h
        vu[x, :, tile] = v
        u2[x, :, tile] = (
            2.0 * c - u[0, x, :, tile] + operate(model, x, tile, h, v, m)
            + plane[1, :, tile]
        )

    def emit_b(x, t, h, v, m, c):
        tile = pl.ds(128 * t, 128)
        hb[x, :, tile] = h
        vb[x, :, tile] = v
        b2[x, :, tile] = (
            2.0 * c + operate(model, x, tile, h, v, m)
            + (q1[x, :, tile] * hu[x, :, tile] + q2[x, :, tile] * vu[x, :, tile])
        )

    derivs(extended(u1, inner, outer, 0), u1.shape[0], ylo, yhi, 0, zmat, emit_u)
    derivs(extended(b1, inner, outer, 1), b1.shape[0], ylo, yhi, 1, zmat, emit_b)
    fields = [u2, b2]
    pack_y(fields, yup, ydn)
    pack_x(fields, inner_out, outer_out)


def counts_kernel(cells, wavelet, source, *rest, size_y, depth):
    out, plane, amounts, place, sems = rest[-5:]
    copies = [
        pltpu.make_async_copy(wavelet, amounts, sems.at[0]),
        pltpu.make_async_copy(source, place, sems.at[1]),
    ]
    for copy in copies:
        copy.start()
    nx, ny = out.shape[0], out.shape[1]
    gx, gy = lax.axis_index("gx"), lax.axis_index("gy")
    index = cells[...]
    cx = lax.div(index, size_y * depth) - gx * nx
    cy = lax.rem(lax.div(index, depth), size_y) - gy * ny
    cz = lax.rem(index, depth)
    inside = (cx >= 0) & (cx < nx) & (cy >= 0) & (cy < ny)
    at = jnp.where(inside, cx * ny + cy, -1)
    n = index.shape[1]
    left = jnp.where(lax.broadcasted_iota(jnp.int32, (nx * ny, n), 0) == at, 1.0, 0.0).astype(BF16)
    right = jnp.where(lax.broadcasted_iota(jnp.int32, (depth, n), 0) == cz, 1.0, 0.0).astype(BF16)
    total = lax.dot_general(left, right, (((1,), (1,)), ((), ())), preferred_element_type=F32)
    out[...] = total.reshape(nx, ny, depth)
    for copy in copies:
        copy.wait()
    cell = lax.broadcasted_iota(jnp.int32, (ny, depth), 1)
    for step in range(plane.shape[0]):
        plane[step] = jnp.where(cell == place[0], amounts[0, step], 0.0)


def adjoint_kernel(
    zmat, l, l1, d1, b1, q1, q2, counts, hu, vu, hb, vb, u2, b2, ylo, yhi, inner, outer,
    speed, epsilon, delta, tilt, l2, d2, a1, c1, hl, vl,
):
    model = (speed, epsilon, delta, tilt)

    def emit_l(x, t, h, v, m, c):
        tile = pl.ds(128 * t, 128)
        hl[x, :, tile] = h
        vl[x, :, tile] = v
        l2[x, :, tile] = 2.0 * c - l[0, x, :, tile] + operate(model, x, tile, h, v, m)

    def emit_d(x, t, h, v, m, c):
        tile = pl.ds(128 * t, 128)
        d2[x, :, tile] = (
            2.0 * c + operate(model, x, tile, h, v, m)
            + (q1[x, :, tile] * hl[x, :, tile] + q2[x, :, tile] * vl[x, :, tile])
            + counts[x, :, tile] * b1[x, :, tile]
        )
        a1[x, :, tile] = hu[x, :, tile] * c + hb[x, :, tile] * l1[x, :, tile]
        c1[x, :, tile] = vu[x, :, tile] * c + vb[x, :, tile] * l1[x, :, tile]

    derivs(extended(l1, inner, outer, 2), l1.shape[0], ylo, yhi, 0, zmat, emit_l)
    derivs(extended(d1, inner, outer, 3), d1.shape[0], ylo, yhi, 1, zmat, emit_d)

    for field, other in ((u2, d2), (b2, l2)):

        def add(x, t, v, other=other):
            tile = pl.ds(128 * t, 128)
            c1[x, :, tile] = c1[x, :, tile] + v * other[x, :, tile]

        second_z(field, zmat, add)


def image_kernel(
    u2, b2, ylo, yhi, inner, outer, l2, d2, a1, c1, near, far, opposite, beside, total, chunks,
):
    fields = [extended(w, inner, outer, f) for f, w in enumerate((u2, b2))]
    nx = u2.shape[0]
    for x in range(nx):
        hu, hb = (
            lateral(w, x, edge_rows(ylo, yhi, x, f, nx // 2), False)[0] for f, w in enumerate(fields)
        )
        for t in (0, 1):
            tile = pl.ds(128 * t, 128)
            total[x, :, tile] = a1[x, :, tile] + hu[t] * d2[x, :, tile] + hb[t] * l2[x, :, tile]
    lane = lanes()
    group = nx // 4
    for i in range(group):
        for f, array in enumerate((total, c1)):
            for t in (0, 1):
                parts = [array[g * group + i, :, pl.ds(128 * t, 128)] for g in range(4)]
                for k in range(4):
                    a, b, c, d = (
                        pltpu.roll(part, (32 * (g - k)) % 128, 1) if g != k else part
                        for g, part in enumerate(parts)
                    )
                    chunks[4 * t + k, f * group + i] = jnp.where(
                        lane < 32, a, jnp.where(lane < 64, b, jnp.where(lane < 96, c, d))
                    )
    shot = lax.axis_index("shot")
    y, xh = shot // 2, lax.rem(shot, 2)

    def chunk_at(there, same):
        return chunks[there * 2 + (xh if same else 1 - xh)]

    inner_y, outer_y = neighbour(y, False), neighbour(y, True)

    for out, wanted in (
        (near, ((y, True), (y, False))),
        (far, ((inner_y, True), (outer_y, True))),
        (opposite, ((y ^ 2, True), (y ^ 2, False))),
        (beside, ((inner_y, False), (outer_y, False))),
    ):
        for i, (there, same) in enumerate(wanted):
            out[i] = chunk_at(there, same)


def add_kernel(here, arrived, *outs):
    for i, out in enumerate(outs):
        out[...] = here[i] + arrived[i]


def sum_kernel(speed, epsilon, delta, own, other, up, down, out):
    group = out.shape[1] // 4
    tile, shift = own_depth(lax.axis_index("shot"))
    for i in range(group):
        sums = []
        for f in (0, 1):
            j = f * group + i
            sums.append((own[j] + other[j]) + (up[j] + down[j]))
        for g in range(4):
            x = g * group + i
            a, c = (pltpu.roll(v, (128 - 32 * g) % 128, 1) if g else v for v in sums)
            s, e, d = (pltpu.roll(w[x, :, tile], shift, 1) for w in (speed, epsilon, delta))
            out[0, x] = (e * a + d * c)[:, 0:32]
            out[1, x] = (s * a)[:, 0:32]
            out[2, x] = (s * c)[:, 0:32]


def per_device(
    speed, epsilon, delta, tilt, perturbation, forward_prev, forward_now, adjoint_prev, adjoint_now,
    wavelet, source_cell, receiver_cells,
):
    nx, ny, nz = speed.shape
    whole = (nx, ny, nz)
    half_rows = (nx // 2, ny, nz)
    layers = [half_rows] * 2 + [(4, ny, nz)] * 2
    packed = (nx // 2, ny, 128)
    model = (speed, epsilon, delta, tilt)

    def exchange_y(inner, outer):
        outer = outer_y(outer)
        return pairs(inner, "gy"), outer

    def exchange_x(inner, outer):
        outer = pairs(outer, "gx", True)
        return pairs(inner, "gx"), outer

    now = (forward_now[0], adjoint_now[0])
    (half,) = call(
        functools.partial(chunk_kernel, which=1),
        [(nx // 4, ny, 128)],
        (perturbation, speed, epsilon),
        [pltpu.VMEM((nx, ny, 128), F32)] * 2,
        name="half_chunk",
    )
    sent = pl.pallas_call(
        first_x_kernel,
        out_shape=[jax.ShapeDtypeStruct((4, ny, nz), F32)] * 2,
        in_specs=[pl.BlockSpec((8, ny, nz), lambda i, at=at: (at, 0, 0)) for at in (0, 0, nx // 8 - 1, nx // 8 - 1)],
        out_specs=[pl.BlockSpec((4, ny, nz), lambda i: (0, 0, 0))] * 2,
        grid=(1,),
        compiler_params=pltpu.CompilerParams(vmem_limit_bytes=LIMIT),
        name="layers_x",
    )(*now, *now)
    x0 = exchange_x(*sent)
    (mine,) = call(
        functools.partial(chunk_kernel, which=2),
        [packed],
        (perturbation, speed, delta, half),
        [pltpu.VMEM((nx, ny, 128), F32)] * 2,
        name="chunk",
    )
    partner, inner, outer = across(mine), beside_y(mine), beside_y(mine, True)
    pair = jnp.concatenate([mine, partner], axis=0)
    *sent, zmat = call(
        first_y_kernel, layers[:2] + [((2, nz, nz), BF16)], now, after=(pair, *x0), name="layers_y"
    )
    y0 = exchange_y(*sent)
    opposite = opposite_y(pair)
    beside = across(jnp.concatenate([inner, outer], axis=0))
    steps = wavelet.shape[1]
    counts, plane = call(
        functools.partial(counts_kernel, size_y=ny * lax.axis_size("gy"), depth=nz),
        [whole, (steps, ny, nz)],
        (receiver_cells,),
        [pltpu.SMEM((1, steps), F32), pltpu.SMEM((1,), jnp.int32), pltpu.SemaphoreType.DMA((2,))],
        after=(wavelet, source_cell, pair, *sent),
        name="counts",
    )
    u1, l1, hu0, vu0, hl0, vl0 = call(
        first_kernel,
        [whole] * 6,
        (plane, zmat, forward_now, forward_prev, adjoint_now, adjoint_prev) + y0 + x0 + model,
        name="first",
    )
    q1, q2, b1, d1, yup, ydn, inner_out, outer_out = call(
        born_kernel,
        [whole] * 4 + layers[:2] + [(8, ny, nz)] * 2,
        (mine, partner, inner, outer, opposite, beside, u1, l1, hu0, vu0, hl0, vl0),
        [pltpu.VMEM((8, nx // 2, ny, 128), F32)],
        name="born",
    )
    y_ub = exchange_y(yup, ydn)
    x1 = exchange_x(inner_out, outer_out)
    y_ld = exchange_y(*call(y_kernel, layers[:2], (l1, d1), name="adjoint_y"))
    u2, b2, hu1, vu1, hb1, vb1, yup, ydn, inner_out, outer_out = call(
        second_kernel,
        [whole] * 6 + layers,
        (plane, zmat, forward_now, u1, b1, q1, q2) + y_ub + x1 + model,
        name="second",
    )
    halo = exchange_y(yup, ydn) + exchange_x(inner_out, outer_out)
    l2, d2, a1, c1 = call(
        adjoint_kernel,
        [whole] * 4,
        (zmat, adjoint_now, l1, d1, b1, q1, q2, counts, hu1, vu1, hb1, vb1, u2, b2) + y_ld + x1 + model,
        [pltpu.VMEM(whole, F32), pltpu.VMEM(whole, F32)],
        name="adjoint",
    )
    near, far, opposite, beside = call(
        image_kernel,
        [(2,) + packed] * 4,
        (u2, b2) + halo + (l2, d2, a1, c1),
        [pltpu.VMEM(whole, F32), pltpu.VMEM((8,) + packed, F32)],
        name="image",
    )
    own, other = call(add_kernel, [packed] * 2, (near, opposite_y(opposite)), name="add_opposite")
    inner, outer = call(add_kernel, [packed] * 2, (far, across(beside)), name="add_beside")
    (out,) = call(
        sum_kernel,
        [(3, nx, ny, nz // 8)],
        model[:3] + (own, across(other), beside_y(inner), beside_y(outer, True)),
        name="sum",
    )
    return out


def solution(mesh):
    placed = (
        P("gx", "gy", None),
        P("gx", "gy", None),
        P("gx", "gy", None),
        P("gx", "gy", None),
        P(None, "gx", "gy", "shot"),
        P("shot", "gx", "gy", None),
        P("shot", "gx", "gy", None),
        P("shot", "gx", "gy", None),
        P("shot", "gx", "gy", None),
        P("shot", None),
        P("shot"),
        P("shot", None),
    )
    return jax.shard_map(
        per_device,
        mesh=mesh,
        in_specs=placed,
        out_specs=P(None, "gx", "gy", "shot"),
        check_vma=False,
    )
```

```python
import functools

import jax
import jax.numpy as jnp
from jax import lax
from jax.experimental import pallas as pl
from jax.experimental.pallas import tpu as pltpu
from jax.sharding import PartitionSpec as P

F32 = jnp.float32
BF16 = jnp.bfloat16
GROUP = 24
LIMIT = 24 * 1024 * 1024

S0, S1, S2 = -2.5, 4.0 / 3.0, -1.0 / 12.0
D1, D2 = 2.0 / 3.0, -1.0 / 12.0


def call(kernel, outs, ins, scratch=(), after=(), name=None):
    places = [pltpu.VMEM] * len(ins) + [pl.ANY] * len(after)
    typed = [out if out[-1] is BF16 else (out, F32) for out in outs]
    return pl.pallas_call(
        kernel,
        out_shape=[jax.ShapeDtypeStruct(*out) for out in typed],
        in_specs=[pl.BlockSpec(memory_space=place) for place in places],
        out_specs=[pl.BlockSpec(memory_space=pltpu.VMEM)] * len(outs),
        scratch_shapes=list(scratch),
        compiler_params=pltpu.CompilerParams(vmem_limit_bytes=LIMIT),
        name=name,
    )(*ins, *after)


def pairs(value, axis, outer=False):
    n = lax.axis_size(axis)
    other = [i ^ 1 if not outer else (((i + 1) % n ^ 1) - 1) % n for i in range(n)]
    return lax.ppermute(value, axis, list(enumerate(other)))


def outer_y(value):
    nx, ny = lax.axis_size("gx"), lax.axis_size("gy")
    swaps = []
    for x in range(nx):
        for y in range(ny):
            there = (x ^ 1, y) if y in (0, ny - 1) else (x, ((y + 1) ^ 1) - 1)
            swaps.append((x * ny + y, there[0] * ny + there[1]))
    return lax.ppermute(value, ("gx", "gy"), swaps)


def across(value):
    return lax.ppermute(value, "shot", [(i, i ^ 1) for i in range(8)])


def opposite_y(value):
    return lax.ppermute(value, "shot", [(i, (i + 4) % 8) for i in range(8)])


def beside_y(value, outer=False):
    return lax.ppermute(value, "shot", [(i, neighbour(i // 2, outer) * 2 + i % 2) for i in range(8)])


def neighbour(y, outer):
    return (y ^ 1) if not outer else (((y + 1) & 3) ^ 1) + 3 & 3


def rows():
    return lax.broadcasted_iota(jnp.int32, (8, 128), 0)


def lanes():
    return lax.broadcasted_iota(jnp.int32, (8, 128), 1)


def even(axis):
    return lax.rem(lax.axis_index(axis), 2) == 0


def pack_y(fields, inner, outer):
    row = rows()
    nx = fields[0].shape[0]
    base = jnp.where(even("gy"), 6, 0)
    for out, base in ((inner, base), (outer, 6 - base)):
        for i in range(nx // 2):
            for h in (0, 128):
                tile = pl.ds(h, 128)
                acc = None
                for piece in (0, 1):
                    for f, field in enumerate(fields):
                        at = 4 * piece + 2 * f
                        value = pltpu.roll(field[i + piece * (nx // 2), :, tile], lax.rem(at + 8 - base, 8), 0)
                        acc = value if acc is None else jnp.where(row >= at, value, acc)
                out[i, :, tile] = acc


def face_x(first, last, inner, outer, f):
    at_even = even("gx")
    inner[2 * f : 2 * f + 2] = jnp.where(at_even, last, first)
    outer[2 * f : 2 * f + 2] = jnp.where(at_even, first, last)


def pack_x(fields, inner, outer):
    for f, field in enumerate(fields):
        n = field.shape[0]
        face_x(field[0:2], field[n - 2 : n], inner, outer, f)


def extended(field, inner, outer, f):
    n = field.shape[0]
    gx, at_even = lax.axis_index("gx"), even("gx")
    inner, outer = inner[2 * f : 2 * f + 2], outer[2 * f : 2 * f + 2]
    before = jnp.where(gx > 0, jnp.where(at_even, outer, inner), 0.0)
    after = jnp.where(gx < lax.axis_size("gx") - 1, jnp.where(at_even, inner, outer), 0.0)

    def slab(x, t):
        if 0 <= x < n:
            return field[x, :, pl.ds(128 * t, 128)]
        return (before[x + 2] if x < 0 else after[x - n])[:, 128 * t : 128 * t + 128]

    return slab


def edge_rows(inner, outer, x, f, half):
    row = rows()
    gy, n = lax.axis_index("gy"), lax.axis_size("gy")
    low = jnp.where(even("gy"), 0, 6)
    from_inner = (row >= low) & (row < low + 2)
    from_outer = (row >= 6 - low) & (row < 8 - low) & (gy > 0) & (gy < n - 1)
    i, at = x % half, 4 * (x // half) + 2 * f
    out = []
    for t in (0, 1):
        tile = pl.ds(128 * t, 128)
        near = pltpu.roll(inner[i, :, tile], lax.rem(low + 8 - at, 8), 0)
        far = pltpu.roll(outer[i, :, tile], lax.rem(14 - low - at, 8), 0)
        out.append(jnp.where(from_inner, near, jnp.where(from_outer, far, 0.0)))
    return out


def along_z(values, matrix):
    total = None
    for _ in range(3):
        part = values.astype(BF16)
        values = values - part.astype(F32)
        term = jnp.dot(part, matrix, preferred_element_type=F32)
        total = term if total is None else total + term
    return total


def lateral(slab, x, edge, slope=True):
    row = rows()
    horizontal, slopes, centre = [], [], []
    for t in (0, 1):
        c, xl, xh, xl2, xh2 = (slab(x + k, t) for k in (0, -1, 1, -2, 2))
        e = edge[t]
        yl = pltpu.roll(jnp.where(row == 7, e, c), 1, 0)
        yl2 = pltpu.roll(jnp.where(row >= 6, e, c), 2, 0)
        yh = pltpu.roll(jnp.where(row == 0, e, c), 7, 0)
        yh2 = pltpu.roll(jnp.where(row <= 1, e, c), 6, 0)
        horizontal.append(2.0 * S0 * c + S1 * ((xl + xh) + (yl + yh)) + S2 * ((xl2 + xh2) + (yl2 + yh2)))
        if slope:
            slopes.append((D1 / 12.0) * ((xh - xl) + (yh - yl)) + (D2 / 12.0) * ((xh2 - xl2) + (yh2 - yl2)))
        centre.append(c)
    return horizontal, slopes, centre


def slabs(lists):
    return jnp.concatenate([jnp.concatenate(pair, axis=1) for pair in lists], axis=0)


def derivs(slab, nx, before, after, f, zmat, emit):
    for at in range(0, nx, GROUP):
        found = [lateral(slab, x, edge_rows(before, after, x, f, nx // 2)) for x in range(at, at + GROUP)]
        vertical = along_z(slabs([c for _, _, c in found]), zmat[0]) * (1.0 / 12.0)
        mixed = along_z(slabs([s for _, s, _ in found]), zmat[1])
        for j, (horizontal, _, centre) in enumerate(found):
            for t in (0, 1):
                part = (slice(8 * j, 8 * j + 8), slice(128 * t, 128 * t + 128))
                emit(at + j, t, horizontal[t], vertical[part], mixed[part], centre[t])


def second_z(field, zmat, emit):
    for at in range(0, field.shape[0], GROUP):
        vertical = along_z(field[at : at + GROUP].reshape(GROUP * 8, field.shape[2]), zmat[0]) * (1.0 / 12.0)
        for j in range(GROUP):
            for t in (0, 1):
                emit(at + j, t, vertical[8 * j : 8 * j + 8, 128 * t : 128 * t + 128])


def operate(model, x, tile, h, v, m):
    s, e, d, k = (w[x, :, tile] for w in model)
    return s * (e * h + d * v) + k * m


def z_matrices(out):
    shape = out.shape[1:]
    offset = lax.broadcasted_iota(jnp.int32, shape, 0) - lax.broadcasted_iota(jnp.int32, shape, 1)
    far = jnp.abs(offset)
    second = jnp.where(far == 0, -30.0, jnp.where(far == 1, 16.0, jnp.where(far == 2, -1.0, 0.0)))
    first = jnp.where(far == 1, 8.0, jnp.where(far == 2, -1.0, 0.0))
    out[0] = second.astype(BF16)
    out[1] = jnp.where(offset > 0, first, -first).astype(BF16)


def own_depth(shot):
    tile = pl.ds(pl.multiple_of((shot // 4) * 128, 128), 128)
    return tile, lax.rem(128 - 32 * lax.rem(shot, 4), 128)


def chunk_kernel(p, speed, other, *rest, which):
    before, (chunk, first, second) = rest[:-3], rest[-3:]
    first[:, :, 0:32] = p[0]
    second[:, :, 0:32] = p[which]
    tile, shift = own_depth(lax.axis_index("shot"))
    lane = lanes()
    group = first.shape[0] // 4
    start = 0
    if before:
        start = group
        chunk[0:group] = before[0][...]
    for i in range(group):
        parts = []
        for g in range(4):
            x = g * group + i
            s, e = (pltpu.roll(w[x, :, tile], shift, 1) for w in (speed, other))
            q = first[x] * e + s * second[x]
            parts.append(pltpu.roll(q, 32 * g, 1) if g else q)
        a, b, c, d = parts
        chunk[start + i] = jnp.where(lane < 32, a, jnp.where(lane < 64, b, jnp.where(lane < 96, c, d)))


def first_x_kernel(u_first, l_first, u_last, l_last, inner, outer):
    for f, (first, last) in enumerate(((u_first, u_last), (l_first, l_last))):
        face_x(first[0:2], last[6:8], inner, outer, f)


def first_y_kernel(u, l, *rest):
    up, down, zmat = rest[-3:]
    pack_y([u, l], up, down)
    z_matrices(zmat)


def y_kernel(a, b, up, down):
    pack_y([a, b], up, down)


def first_kernel(
    plane, zmat, u, um, l, lm, ylo, yhi, inner, outer, speed, epsilon, delta, tilt,
    u1, l1, hu, vu, hl, vl,
):
    model = (speed, epsilon, delta, tilt)
    for f, (w, prev, new, h_out, v_out) in enumerate(((u, um, u1, hu, vu), (l, lm, l1, hl, vl))):

        def emit(x, t, h, v, m, c, f=f, prev=prev, new=new, h_out=h_out, v_out=v_out):
            tile = pl.ds(128 * t, 128)
            h_out[x, :, tile] = h
            v_out[x, :, tile] = v
            value = 2.0 * c - prev[0, x, :, tile] + operate(model, x, tile, h, v, m)
            if f == 0:
                value = value + plane[0, :, tile]
            new[x, :, tile] = value

        slab = extended(w.at[0], inner, outer, f)
        derivs(slab, w.shape[1], ylo, yhi, f, zmat, emit)


def born_kernel(
    mine, partner, inner, outer, opposite, beside, u1, l1, hu, vu, hl, vl, q1, q2, b1, d1, yup, ydn, inner_out, outer_out, chunks,
):
    shot = lax.axis_index("shot")
    y, xh = shot // 2, lax.rem(shot, 2)
    group = hu.shape[0] // 4
    n = 2 * group
    for there, same, other in (
        (y, mine[...], partner[...]),
        (neighbour(y, False), inner[...], beside[0:n]),
        (neighbour(y, True), outer[...], beside[n : 2 * n]),
        (y ^ 2, opposite[0:n], opposite[n : 2 * n]),
    ):
        chunks[there * 2 + xh] = same
        chunks[there * 2 + 1 - xh] = other
    lane = lanes()
    for x in range(4 * group):
        g, i = x // group, x % group
        for t in (0, 1):
            tile = pl.ds(128 * t, 128)
            both = []
            for f in (0, 1):
                parts = []
                for k in range(4):
                    part = chunks[4 * t + k, f * group + i]
                    parts.append(pltpu.roll(part, (32 * (k - g)) % 128, 1) if k != g else part)
                a, b, c, d = parts
                both.append(jnp.where(lane < 32, a, jnp.where(lane < 64, b, jnp.where(lane < 96, c, d))))
            q1[x, :, tile], q2[x, :, tile] = both
            b1[x, :, tile] = both[0] * hu[x, :, tile] + both[1] * vu[x, :, tile]
            d1[x, :, tile] = both[0] * hl[x, :, tile] + both[1] * vl[x, :, tile]
    pack_y([u1, b1], yup, ydn)
    pack_x([u1, b1, l1, d1], inner_out, outer_out)


def second_kernel(
    plane, zmat, u, u1, b1, q1, q2, ylo, yhi, inner, outer, speed, epsilon, delta, tilt,
    u2, b2, hu, vu, hb, vb, yup, ydn, inner_out, outer_out,
):
    model = (speed, epsilon, delta, tilt)

    def emit_u(x, t, h, v, m, c):
        tile = pl.ds(128 * t, 128)
        hu[x, :, tile] = h
        vu[x, :, tile] = v
        u2[x, :, tile] = (
            2.0 * c - u[0, x, :, tile] + operate(model, x, tile, h, v, m)
            + plane[1, :, tile]
        )

    def emit_b(x, t, h, v, m, c):
        tile = pl.ds(128 * t, 128)
        hb[x, :, tile] = h
        vb[x, :, tile] = v
        b2[x, :, tile] = (
            2.0 * c + operate(model, x, tile, h, v, m)
            + (q1[x, :, tile] * hu[x, :, tile] + q2[x, :, tile] * vu[x, :, tile])
        )

    derivs(extended(u1, inner, outer, 0), u1.shape[0], ylo, yhi, 0, zmat, emit_u)
    derivs(extended(b1, inner, outer, 1), b1.shape[0], ylo, yhi, 1, zmat, emit_b)
    fields = [u2, b2]
    pack_y(fields, yup, ydn)
    pack_x(fields, inner_out, outer_out)


def counts_kernel(cells, wavelet, source, *rest, size_y, depth):
    out, plane, amounts, place, sems = rest[-5:]
    copies = [
        pltpu.make_async_copy(wavelet, amounts, sems.at[0]),
        pltpu.make_async_copy(source, place, sems.at[1]),
    ]
    for copy in copies:
        copy.start()
    nx, ny = out.shape[0], out.shape[1]
    gx, gy = lax.axis_index("gx"), lax.axis_index("gy")
    index = cells[...]
    cx = lax.div(index, size_y * depth) - gx * nx
    cy = lax.rem(lax.div(index, depth), size_y) - gy * ny
    cz = lax.rem(index, depth)
    inside = (cx >= 0) & (cx < nx) & (cy >= 0) & (cy < ny)
    at = jnp.where(inside, cx * ny + cy, -1)
    n = index.shape[1]
    left = jnp.where(lax.broadcasted_iota(jnp.int32, (nx * ny, n), 0) == at, 1.0, 0.0).astype(BF16)
    right = jnp.where(lax.broadcasted_iota(jnp.int32, (depth, n), 0) == cz, 1.0, 0.0).astype(BF16)
    total = lax.dot_general(left, right, (((1,), (1,)), ((), ())), preferred_element_type=F32)
    out[...] = total.reshape(nx, ny, depth)
    for copy in copies:
        copy.wait()
    cell = lax.broadcasted_iota(jnp.int32, (ny, depth), 1)
    for step in range(plane.shape[0]):
        plane[step] = jnp.where(cell == place[0], amounts[0, step], 0.0)


def adjoint_kernel(
    zmat, l, l1, d1, b1, q1, q2, counts, hu, vu, hb, vb, u2, b2, ylo, yhi, inner, outer,
    speed, epsilon, delta, tilt, l2, d2, a1, c1, hl, vl,
):
    model = (speed, epsilon, delta, tilt)

    def emit_l(x, t, h, v, m, c):
        tile = pl.ds(128 * t, 128)
        hl[x, :, tile] = h
        vl[x, :, tile] = v
        l2[x, :, tile] = 2.0 * c - l[0, x, :, tile] + operate(model, x, tile, h, v, m)

    def emit_d(x, t, h, v, m, c):
        tile = pl.ds(128 * t, 128)
        d2[x, :, tile] = (
            2.0 * c + operate(model, x, tile, h, v, m)
            + (q1[x, :, tile] * hl[x, :, tile] + q2[x, :, tile] * vl[x, :, tile])
            + counts[x, :, tile] * b1[x, :, tile]
        )
        a1[x, :, tile] = hu[x, :, tile] * c + hb[x, :, tile] * l1[x, :, tile]
        c1[x, :, tile] = vu[x, :, tile] * c + vb[x, :, tile] * l1[x, :, tile]

    derivs(extended(l1, inner, outer, 2), l1.shape[0], ylo, yhi, 0, zmat, emit_l)
    derivs(extended(d1, inner, outer, 3), d1.shape[0], ylo, yhi, 1, zmat, emit_d)

    for field, other in ((u2, d2), (b2, l2)):

        def add(x, t, v, other=other):
            tile = pl.ds(128 * t, 128)
            c1[x, :, tile] = c1[x, :, tile] + v * other[x, :, tile]

        second_z(field, zmat, add)


def image_kernel(
    u2, b2, ylo, yhi, inner, outer, l2, d2, a1, c1, near, far, opposite, beside, total, chunks,
):
    fields = [extended(w, inner, outer, f) for f, w in enumerate((u2, b2))]
    nx = u2.shape[0]
    for x in range(nx):
        hu, hb = (
            lateral(w, x, edge_rows(ylo, yhi, x, f, nx // 2), False)[0] for f, w in enumerate(fields)
        )
        for t in (0, 1):
            tile = pl.ds(128 * t, 128)
            total[x, :, tile] = a1[x, :, tile] + hu[t] * d2[x, :, tile] + hb[t] * l2[x, :, tile]
    lane = lanes()
    group = nx // 4
    for i in range(group):
        for f, array in enumerate((total, c1)):
            for t in (0, 1):
                parts = [array[g * group + i, :, pl.ds(128 * t, 128)] for g in range(4)]
                for k in range(4):
                    a, b, c, d = (
                        pltpu.roll(part, (32 * (g - k)) % 128, 1) if g != k else part
                        for g, part in enumerate(parts)
                    )
                    chunks[4 * t + k, f * group + i] = jnp.where(
                        lane < 32, a, jnp.where(lane < 64, b, jnp.where(lane < 96, c, d))
                    )
    shot = lax.axis_index("shot")
    y, xh = shot // 2, lax.rem(shot, 2)

    def chunk_at(there, same):
        return chunks[there * 2 + (xh if same else 1 - xh)]

    inner_y, outer_y = neighbour(y, False), neighbour(y, True)

    for out, wanted in (
        (near, ((y, True), (y, False))),
        (far, ((inner_y, True), (outer_y, True))),
        (opposite, ((y ^ 2, True), (y ^ 2, False))),
        (beside, ((inner_y, False), (outer_y, False))),
    ):
        for i, (there, same) in enumerate(wanted):
            out[i] = chunk_at(there, same)


def add_kernel(here, arrived, *outs):
    for i, out in enumerate(outs):
        out[...] = here[i] + arrived[i]


def sum_kernel(speed, epsilon, delta, own, other, up, down, out, values, turned, sems):
    group = values.shape[1] // 4
    tile, shift = own_depth(lax.axis_index("shot"))
    for i in range(group):
        sums = []
        for f in (0, 1):
            j = f * group + i
            sums.append((own[j] + other[j]) + (up[j] + down[j]))
        for g in range(4):
            x = g * group + i
            a, c = (pltpu.roll(v, (128 - 32 * g) % 128, 1) if g else v for v in sums)
            s, e, d = (pltpu.roll(w[x, :, tile], shift, 1) for w in (speed, epsilon, delta))
            values[0, x] = e * a + d * c
            values[1, x] = s * a
            values[2, x] = s * c
    copies = [pltpu.make_async_copy(turned.at[k], out.at[k], sems.at[k]) for k in range(3)]
    for k, copy in enumerate(copies):
        for y in range(turned.shape[1]):
            turned[k, y] = values[k, :, y, 0:32].T
        copy.start()
    for copy in copies:
        copy.wait()


def per_device(
    speed, epsilon, delta, tilt, perturbation, forward_prev, forward_now, adjoint_prev, adjoint_now,
    wavelet, source_cell, receiver_cells,
):
    nx, ny, nz = speed.shape
    whole = (nx, ny, nz)
    half_rows = (nx // 2, ny, nz)
    layers = [half_rows] * 2 + [(4, ny, nz)] * 2
    packed = (nx // 2, ny, 128)
    model = (speed, epsilon, delta, tilt)

    def exchange_y(inner, outer):
        outer = outer_y(outer)
        return pairs(inner, "gy"), outer

    def exchange_x(inner, outer):
        outer = pairs(outer, "gx", True)
        return pairs(inner, "gx"), outer

    now = (forward_now[0], adjoint_now[0])
    (half,) = call(
        functools.partial(chunk_kernel, which=1),
        [(nx // 4, ny, 128)],
        (perturbation, speed, epsilon),
        [pltpu.VMEM((nx, ny, 128), F32)] * 2,
        name="half_chunk",
    )
    sent = pl.pallas_call(
        first_x_kernel,
        out_shape=[jax.ShapeDtypeStruct((4, ny, nz), F32)] * 2,
        in_specs=[pl.BlockSpec((8, ny, nz), lambda i, at=at: (at, 0, 0)) for at in (0, 0, nx // 8 - 1, nx // 8 - 1)],
        out_specs=[pl.BlockSpec((4, ny, nz), lambda i: (0, 0, 0))] * 2,
        grid=(1,),
        compiler_params=pltpu.CompilerParams(vmem_limit_bytes=LIMIT),
        name="layers_x",
    )(*now, *now)
    x0 = exchange_x(*sent)
    (mine,) = call(
        functools.partial(chunk_kernel, which=2),
        [packed],
        (perturbation, speed, delta, half),
        [pltpu.VMEM((nx, ny, 128), F32)] * 2,
        name="chunk",
    )
    partner, inner, outer = across(mine), beside_y(mine), beside_y(mine, True)
    pair = jnp.concatenate([mine, partner], axis=0)
    *sent, zmat = call(
        first_y_kernel, layers[:2] + [((2, nz, nz), BF16)], now, after=(pair, *x0), name="layers_y"
    )
    y0 = exchange_y(*sent)
    opposite = opposite_y(pair)
    beside = across(jnp.concatenate([inner, outer], axis=0))
    steps = wavelet.shape[1]
    counts, plane = call(
        functools.partial(counts_kernel, size_y=ny * lax.axis_size("gy"), depth=nz),
        [whole, (steps, ny, nz)],
        (receiver_cells,),
        [pltpu.SMEM((1, steps), F32), pltpu.SMEM((1,), jnp.int32), pltpu.SemaphoreType.DMA((2,))],
        after=(wavelet, source_cell, pair, *sent),
        name="counts",
    )
    u1, l1, hu0, vu0, hl0, vl0 = call(
        first_kernel,
        [whole] * 6,
        (plane, zmat, forward_now, forward_prev, adjoint_now, adjoint_prev) + y0 + x0 + model,
        name="first",
    )
    q1, q2, b1, d1, yup, ydn, inner_out, outer_out = call(
        born_kernel,
        [whole] * 4 + layers[:2] + [(8, ny, nz)] * 2,
        (mine, partner, inner, outer, opposite, beside, u1, l1, hu0, vu0, hl0, vl0),
        [pltpu.VMEM((8, nx // 2, ny, 128), F32)],
        name="born",
    )
    y_ub = exchange_y(yup, ydn)
    x1 = exchange_x(inner_out, outer_out)
    y_ld = exchange_y(*call(y_kernel, layers[:2], (l1, d1), name="adjoint_y"))
    u2, b2, hu1, vu1, hb1, vb1, yup, ydn, inner_out, outer_out = call(
        second_kernel,
        [whole] * 6 + layers,
        (plane, zmat, forward_now, u1, b1, q1, q2) + y_ub + x1 + model,
        name="second",
    )
    halo = exchange_y(yup, ydn) + exchange_x(inner_out, outer_out)
    l2, d2, a1, c1 = call(
        adjoint_kernel,
        [whole] * 4,
        (zmat, adjoint_now, l1, d1, b1, q1, q2, counts, hu1, vu1, hb1, vb1, u2, b2) + y_ld + x1 + model,
        [pltpu.VMEM(whole, F32), pltpu.VMEM(whole, F32)],
        name="adjoint",
    )
    near, far, opposite, beside = call(
        image_kernel,
        [(2,) + packed] * 4,
        (u2, b2) + halo + (l2, d2, a1, c1),
        [pltpu.VMEM(whole, F32), pltpu.VMEM((8,) + packed, F32)],
        name="image",
    )
    own, other = call(add_kernel, [packed] * 2, (near, opposite_y(opposite)), name="add_opposite")
    inner, outer = call(add_kernel, [packed] * 2, (far, across(beside)), name="add_beside")
    turned = (3, ny, nz // 8, nx)
    out = pl.pallas_call(
        sum_kernel,
        out_shape=jax.ShapeDtypeStruct(turned, F32),
        in_specs=[pl.BlockSpec(memory_space=pltpu.VMEM)] * 7,
        out_specs=pl.BlockSpec(memory_space=pl.ANY),
        scratch_shapes=[
            pltpu.VMEM((3, nx, ny, 128), F32),
            pltpu.VMEM(turned, F32),
            pltpu.SemaphoreType.DMA((3,)),
        ],
        compiler_params=pltpu.CompilerParams(vmem_limit_bytes=LIMIT),
        name="sum",
    )(*(model[:3] + (own, across(other), beside_y(inner), beside_y(outer, True))))
    return jnp.transpose(out, (0, 3, 1, 2))


def solution(mesh):
    placed = (
        P("gx", "gy", None),
        P("gx", "gy", None),
        P("gx", "gy", None),
        P("gx", "gy", None),
        P(None, "gx", "gy", "shot"),
        P("shot", "gx", "gy", None),
        P("shot", "gx", "gy", None),
        P("shot", "gx", "gy", None),
        P("shot", "gx", "gy", None),
        P("shot", None),
        P("shot"),
        P("shot", None),
    )
    return jax.shard_map(
        per_device,
        mesh=mesh,
        in_specs=placed,
        out_specs=P(None, "gx", "gy", "shot"),
        check_vma=False,
    )
```
